128 devices in a mesh: lat: 8 (over z, core), lon: 16 (over y, x).
Axes of the slice: x: 4, y: 4, z: 4, core: 2. Of those that a mesh axis runs over, the one named last changes fastest.
Arguments:
- increment: float32 [8, 16, 128, 2048], P(None, None, 'lat', 'lon'), may hold values from -6 to 6
- courant: float32 [2, 16, 128, 2048], P(None, None, 'lat', 'lon'), may hold values from -0.6 to 0.6
- spectra: bfloat16 [147456, 8461], P(('lat', 'lon')), may hold values from -6 to 6
- components: bfloat16 [300, 8461], replicated, may hold values from -0.0625 to 0.0625
- jacobian: bfloat16 [128, 300], replicated, may hold values from -0.5 to 0.5
- obs_weight: float32 [300], replicated, may hold values from 0.3 to 3
- tile_target: int32 [147456, 1], P(('lat', 'lon')), may hold values from 0 to 127; in each aligned block of 1152 rows (0 to 1151, 1152 to 2303, ...) at most 18 rows name the same one
- tile_cell: int32 [147456], P(('lat', 'lon')), may hold values from 0 to 2047
Outputs:
- gradient: float32 [8, 16, 128, 2048], P(None, None, 'lat', 'lon')
- departures: bfloat16 [147456, 300], P(('lat', 'lon'))
The draws below stay inside these ranges and needn't reach their ends.
Inputs may be any that keep to these rules, and one draw needn't show every extreme that they name: `tile_target`: among the rows of one device at most 18 name the same tile, a bound that some block reaches of them.
All inputs are finite; a program needn't handle non-finite values.
Results may differ from the reference program's by a relative error of at most 0.0055.
Values may be sent and summed in bfloat16 or wider, within the bound.
No kernel may reach another device: no remote copies, remote signals or barrier semaphores. Data moves between devices by JAX's collectives and lax.ppermute only.
A program may use at most 128 MiB of HBM per device.

```python
import math
import jax
import jax.numpy as jnp
import numpy as np
from jax import lax

TR = 8
LEV = 16
CLAT = 16
CLON = 128
CH = 8461
PC = 300
OBS_DEV = 1152
STEPS = 4
NLAT = 128
NLON = 2048
OBS = 147456
CAP = 18
N_LON = 16
DEVICES = 128


def set_ends(array, stream_key, low, high):
    dims = array.shape
    place = [jax.random.randint(jax.random.fold_in(stream_key, axis), (), 0, dims[axis]) for axis in range(len(dims))]
    array = array.at[tuple(place)].set(low)
    longest = dims.index(max(dims))
    place[longest] = (place[longest] + 1) % dims[longest]
    return array.at[tuple(place)].set(high)


def block_levels(own_key, extent, pieces, smallest, top_value):
    level, own = 1.0, jax.random.fold_in(own_key, 6)
    for axis_at, blocks in pieces:
        heights = jnp.exp(jax.random.uniform(jax.random.fold_in(own, axis_at), (blocks,), jnp.float32, smallest / len(pieces), top_value / len(pieces)))
        level = level * jnp.repeat(heights, extent[axis_at] // blocks).reshape([-1 if axis == axis_at else 1 for axis in range(len(extent))])
    return level


def deal_out(own_key, own, number, rows, count, top, bound, slope):
    ranking = jax.random.permutation(own_key, count)
    crowded, common = load_shares(count, rows * top, bound, slope, True), load_shares(count, rows * top, bound, slope, False)
    places = jnp.arange(count)

    def named(lengths, rotation):
        used = int((lengths > 0).sum())
        fixed = max(1, used // 4)
        moved = fixed + (places - fixed + rotation * (used - fixed)) % max(1, count - fixed)
        return jnp.zeros((count,), jnp.int32).at[ranking[jnp.where(places < fixed, places, moved)]].set(jnp.asarray(lengths, jnp.int32))

    lengths = jnp.where(number % 4 == 0, named(crowded, number // 4), named(common, number - number // 4 - 1))
    mixed = jax.random.permutation(jax.random.fold_in(own, 3), count)
    donor, sink = mixed[0:count // 2 * 2:2], mixed[1:count // 2 * 2:2]
    room = jnp.minimum(lengths[donor] - 1, bound - lengths[sink]) // 2
    room = jnp.where((donor == ranking[0]) | (sink == ranking[0]) | (lengths[sink] == 0), 0, jnp.maximum(room, 0))
    moved = jax.random.randint(jax.random.fold_in(own, 4), (count // 2,), 0, 1 << 20) % (room + 1)
    lengths = lengths.at[donor].add(-moved).at[sink].add(moved)
    items = jnp.searchsorted(jnp.cumsum(lengths), jnp.arange(rows * top), side="right").astype(jnp.int32)
    listing = items.reshape(top, rows).T
    listing = listing[jax.random.permutation(jax.random.fold_in(own, 1), rows)]
    rotation = jax.random.randint(jax.random.fold_in(own, 2), (rows, 1), 0, top)
    return jnp.take_along_axis(listing, (jnp.arange(top)[None, :] + rotation) % top, axis=1)


def load_shares(amount, total, reach, slope, full):
    weights = [(1 << 20) // math.isqrt(rank ** slope) + 1 for rank in range(1, amount + 1)]
    largest = reach if full else min(reach, max(-(-total // amount), total * weights[0] // sum(weights)))
    least = 1 if total - largest >= amount - 1 else 0
    counts, rest = [largest] + [least] * (amount - 1), total - largest - least * (amount - 1)
    while rest > 0:
        movable = [i for i in range(1, amount) if counts[i] < largest] or [i for i in range(1, amount) if counts[i] < reach]
        mass, remaining = sum([weights[i] for i in movable]), rest
        for i in movable:
            more = min(reach - counts[i], max(1, remaining * weights[i] // mass), rest)
            counts[i] = counts[i] + more
            rest = rest - more
    return np.array(counts)


def scatter_about(key, shape, deviation, limit, pieces=(), dtype=jnp.bfloat16):
    drawn = jax.random.normal(key, shape, jnp.float32) * deviation
    if len(pieces) > 0:
        drawn = block_levels(key, shape, pieces, -0.22, 0.18) * drawn
    return jnp.clip(drawn, min=-limit, max=limit).astype(dtype)


def setup_inputs(seed: int = 0) -> dict:
    arg_keys = jax.random.split(jax.random.key(seed), 9)
    increment = scatter_about(arg_keys[0], (TR, LEV, NLAT, NLON), 1.0, 6.0, ((2, 8), (3, 16)), jnp.float32)
    courant = jnp.clip(jax.random.uniform(arg_keys[1], (2, LEV, NLAT, NLON), jnp.float32, -0.6, 0.6) * block_levels(arg_keys[1], (2, LEV, NLAT, NLON), ((2, 8), (3, 16)), -0.4, 0.0), -0.6, 0.6)
    spectra = scatter_about(arg_keys[2], (OBS, CH), 1.0, 6.0, ((0, 128),))
    components = scatter_about(arg_keys[3], (PC, CH), CH ** -0.5, 0.0625)
    jacobian = scatter_about(arg_keys[4], (TR * LEV, PC), (TR * LEV) ** -0.5, 0.5)
    obs_weight = jnp.clip(jnp.exp(jax.random.uniform(arg_keys[5], (PC,), jnp.float32, math.log(0.3), math.log(3.0))), 0.3, 3.0)
    tile_target_keys = jax.random.split(jax.random.fold_in(arg_keys[6], 1), OBS // OBS_DEV)
    tile_target_turns = jax.random.permutation(jax.random.fold_in(arg_keys[6], 3), OBS // OBS_DEV)
    tile_target = jax.vmap(lambda own, number: deal_out(jax.random.fold_in(arg_keys[6], 2), own, number, OBS_DEV, DEVICES, 1, CAP, 2))(tile_target_keys, tile_target_turns).reshape((OBS, 1))
    tile_cell = set_ends(jax.random.randint(arg_keys[7], (OBS,), 0, CLAT * CLON), jax.random.fold_in(arg_keys[7], 1), 0, (CLAT * CLON) - 1).astype(jnp.int32)
    return {"increment": increment, "courant": courant, "spectra": spectra, "components": components, "jacobian": jacobian, "obs_weight": obs_weight, "tile_target": tile_target, "tile_cell": tile_cell}


def coefficients(pair):
    along = pair[0]
    across = pair[1]
    centre = 1.0 - along * along - across * across
    weight_west = 0.5 * along * (1.0 + along)
    weight_east = -0.5 * along * (1.0 - along)
    weight_south = 0.5 * across * (1.0 + across)
    weight_north = -0.5 * across * (1.0 - across)
    return (centre, weight_west, weight_east, weight_south, weight_north)


def tangent_apply(padded, coefs):
    centre, weight_west, weight_east, weight_south, weight_north = coefs
    result = centre * padded[..., 1:-1, 1:-1] + weight_west * padded[..., 1:-1, :-2]
    result = result + weight_east * padded[..., 1:-1, 2:] + weight_south * padded[..., :-2, 1:-1]
    return result + weight_north * padded[..., 2:, 1:-1]


def adjoint_apply(padded, coefs):
    centre, weight_west, weight_east, weight_south, weight_north = coefs
    result = centre[..., 1:-1, 1:-1] * padded[..., 1:-1, 1:-1]
    result = result + (weight_west * padded)[..., 1:-1, 2:] + (weight_east * padded)[..., 1:-1, :-2]
    result = result + (weight_south * padded)[..., 2:, 1:-1] + (weight_north * padded)[..., :-2, 1:-1]
    return result


def wrap_pad(field):
    widths = [(0, 0)] * (field.ndim - 2) + [(1, 1), (0, 0)]
    field = jnp.pad(field, widths)
    return jnp.concatenate([field[..., -1:], field, field[..., :1]], axis=-1)


def reference(increment, courant, spectra, components, jacobian, obs_weight, tile_target, tile_cell):
    coefs = coefficients(courant)
    state = increment
    for step in range(STEPS):
        state = tangent_apply(wrap_pad(state), coefs)
    blocks = spectra.reshape(-1, OBS_DEV, CH)
    comp_wide = components.astype(jnp.float32)

    def project(block):
        return jnp.dot(block.astype(jnp.float32), comp_wide.T, precision=lax.Precision.HIGHEST)

    scores = lax.map(project, blocks).reshape(-1, PC).astype(jnp.bfloat16)
    target = tile_target[:, 0]
    lat_row = (target // N_LON) * CLAT + tile_cell // CLON
    lon_col = (target % N_LON) * CLON + tile_cell % CLON
    column = state[:, :, lat_row, lon_col].reshape(TR * LEV, -1).astype(jnp.bfloat16)
    jac_wide = jacobian.astype(jnp.float32)
    model = jnp.dot(column.astype(jnp.float32).T, jac_wide, precision=lax.Precision.HIGHEST)
    departures = (obs_weight * (scores.astype(jnp.float32) - model)).astype(jnp.bfloat16)
    terms = jnp.dot(departures.astype(jnp.float32), jac_wide.T, precision=lax.Precision.HIGHEST)
    forcing = jnp.zeros((TR * LEV, NLAT, NLON), jnp.float32).at[:, lat_row, lon_col].add(terms.T)
    forcing = forcing.reshape(TR, LEV, NLAT, NLON)
    wide_coefs = tuple(wrap_pad(item) for item in coefs)
    for step in range(STEPS):
        forcing = adjoint_apply(wrap_pad(forcing), wide_coefs)
    return increment - forcing, departures
```

```python
import jax
import jax.numpy as jnp
from jax import lax
from jax.experimental import pallas as pl
from jax.experimental.pallas import tpu as pltpu
from jax.sharding import PartitionSpec as P

F32 = jnp.float32
BF16 = jnp.bfloat16
TRACERS, LEVELS, ROWS, COLS = 8, 16, 16, 128
FEATS = TRACERS * LEVELS
STEPS = 4
WIDE = ROWS + 2 * STEPS
PARTS = FEATS // 8
WINDS = 2 * LEVELS // 8
CAP = 18
HALF = CAP // 2
SPLIT = 64
VMEM = 56 * 1024 * 1024


def params(**kw):
    return pltpu.CompilerParams(vmem_limit_bytes=VMEM, **kw)


def nn(a, b):
    return lax.dot_general(a, b, (((1,), (0,)), ((), ())), preferred_element_type=F32)


def nt(a, b):
    return lax.dot_general(a, b, (((1,), (1,)), ((), ())), preferred_element_type=F32)


def iota(shape, dim):
    return lax.broadcasted_iota(jnp.int32, shape, dim)


def flipped(a):
    return a.astype(F32).T


def two_parts(a):
    high = a.astype(BF16)
    return high, (a - high.astype(F32)).astype(BF16)


def ranks(target):
    count = target.shape[1]
    tri = (iota((128, 128), 0) <= iota((128, 128), 1)).astype(F32).astype(BF16)
    carry = jnp.zeros((128, 1), F32)
    found = []
    for at in range(0, count, 128):
        hit = (iota((128, 128), 0) == target[:, at : at + 128]).astype(F32)
        upto = nn(hit.astype(BF16), tri) + carry
        carry = upto[:, 127:128]
        found.append(jnp.sum(hit * upto, axis=0, keepdims=True))
    return (jnp.concatenate(found, axis=1) - 1.0).astype(jnp.int32)


def keyed(target, rank):
    late = (rank >= HALF).astype(jnp.int32)
    return 2 * target + late, rank - HALF * late


def key_hits(key, tiles):
    return (iota((2 * tiles, key.shape[1]), 0) == key).astype(F32).astype(BF16)


def picked(hits, rest, slot):
    chosen = jnp.broadcast_to((rest == slot).astype(F32), (16, rest.shape[1])).astype(BF16)
    rows, count = hits.shape
    return (hits.reshape(rows // 16, 16, count) * chosen[None]).reshape(rows, count)


def project_kernel(target, cell, comps, spec, jac_t, weight, scores, send, total):
    step = pl.program_id(0)
    count = target.shape[1]
    tiles = send.shape[0] // 2
    block = spec.shape[1]
    found = nn(comps[...], spec[...]).astype(BF16)
    scores[...] = found
    high, low = two_parts(flipped(jac_t[...]) * weight[...])
    total[:, pl.ds(pl.multiple_of(step * block, block), block)] = nn(high, found) + nn(low, found)

    @pl.when(step == pl.num_programs(0) - 1)
    def _():
        key, rest = keyed(target[...], ranks(target[...]))
        hits = key_hits(key, tiles)
        values = total[:, :count].T.astype(BF16)
        for slot in range(HALF):
            send[:, slot * 128 : slot * 128 + 128] = nn(picked(hits, rest, slot), values).astype(BF16)
        number = cell[...] + 1
        upper = number // SPLIT
        lower = number - upper * SPLIT
        lane = iota((128, count), 0)
        coded = jnp.where(lane == rest, upper, 0) + jnp.where(lane - SPLIT == rest, lower, 0)
        send[:, HALF * 128 :] = nt(hits, coded.astype(F32).astype(BF16)).astype(BF16)


def project(target, cell, comps, spec_t, jac_t, weight, tiles):
    pcs, channels = comps.shape
    count = spec_t.shape[1]
    block = 256
    steps = pl.cdiv(count, block)
    whole = lambda a: pl.BlockSpec(a.shape, lambda i: (0, 0))
    return pl.pallas_call(
        project_kernel,
        grid=(steps,),
        in_specs=[
            whole(target),
            whole(cell),
            whole(comps),
            pl.BlockSpec((channels, block), lambda i: (0, i)),
            whole(jac_t),
            whole(weight),
        ],
        out_specs=[
            pl.BlockSpec((pcs, block), lambda i: (0, i)),
            pl.BlockSpec((2 * tiles, HALF * 128 + 128), lambda i: (0, 0)),
        ],
        out_shape=[
            jax.ShapeDtypeStruct((pcs, count), BF16),
            jax.ShapeDtypeStruct((2 * tiles, HALF * 128 + 128), BF16),
        ],
        scratch_shapes=[pltpu.VMEM((FEATS, steps * block), F32)],
        compiler_params=params(),
        cost_estimate=pl.CostEstimate(
            flops=2 * pcs * channels * count, bytes_accessed=2 * channels * (count + pcs), transcendentals=0
        ),
        name="project",
    )(target, cell, comps, spec_t, jac_t, weight)


def own_part(inc, wind, part, row):
    if part < PARTS:
        return inc[pl.ds(part * 8 * ROWS + row, 8, stride=ROWS), :]
    return wind[pl.ds((part - PARTS) * 8 * ROWS + row, 8, stride=ROWS), :]


def lat_edges_kernel(inc, wind, low, high):
    for at in range(STEPS):
        for part in range(PARTS + WINDS):
            low[at, part * 8 : part * 8 + 8, :] = own_part(inc, wind, part, at)
            high[at, part * 8 : part * 8 + 8, :] = own_part(inc, wind, part, ROWS - STEPS + at)


def lat_edges(inc, wind):
    shape = jax.ShapeDtypeStruct((STEPS, FEATS + 2 * LEVELS, COLS), F32)
    return pl.pallas_call(
        lat_edges_kernel, out_shape=[shape, shape], compiler_params=params(), name="lat_edges"
    )(inc, wind)


def pack_row(parts):
    lane = iota((8, 128), 1) // STEPS
    low = jnp.zeros((8, 128), F32)
    high = low
    for at, part in enumerate(parts):
        low = jnp.where(lane == at, pltpu.roll(part, STEPS * at, 1), low)
        high = jnp.where(lane == at, pltpu.roll(part, (STEPS * at + STEPS) % 128, 1), high)
    return low, high


def lon_edges_kernel(inc, wind, south, north, low, high):
    every = range(PARTS + WINDS)
    for at in range(STEPS):
        for side, first in ((south, 0), (north, ROWS + STEPS)):
            pair = pack_row([side[at, part * 8 : part * 8 + 8, :] for part in every])
            low[first + at], high[first + at] = pair

    def body(row, carry):
        pair = pack_row([own_part(inc, wind, part, row) for part in every])
        low[STEPS + row], high[STEPS + row] = pair
        return carry

    lax.fori_loop(0, ROWS, body, 0)


def lon_edges(inc, wind, south, north):
    shape = jax.ShapeDtypeStruct((WIDE, 8, 128), F32)
    return pl.pallas_call(
        lon_edges_kernel, out_shape=[shape, shape], compiler_params=params(), name="lon_edges"
    )(inc, wind, south, north)


def windows(part, at, west, east):
    lane = iota((8, 128), 1)
    left = pltpu.roll(west, (128 - STEPS * at) % 128, 1)
    right = pltpu.roll(east, (128 - STEPS - STEPS * at) % 128, 1)
    return (
        jnp.where(lane < STEPS, left, pltpu.roll(part, STEPS, 1)),
        jnp.where(lane >= 128 - STEPS, right, pltpu.roll(part, 128 - STEPS, 1)),
    )


def joined(left, right):
    lane = iota((8, 128), 1)
    return jnp.where(lane < 64, pltpu.roll(left, 128 - STEPS, 1), pltpu.roll(right, STEPS, 1))


def put_coefs(coefs, row, wide, inside):
    for side in range(2):
        for half in range(2):
            along = wide[half][side] * inside
            across = wide[2 + half][side] * inside
            at = 2 * side + half
            coefs[row, at, 0] = (1.0 - along * along - across * across) * inside
            coefs[row, at, 1] = 0.5 * along * (1.0 + along)
            coefs[row, at, 2] = -0.5 * along * (1.0 - along)
            coefs[row, at, 3] = 0.5 * across * (1.0 + across)
            coefs[row, at, 4] = -0.5 * across * (1.0 - across)


def tangent_row(now, coefs, row, done):
    for side in range(2):
        for half in range(2):
            weights = [coefs[row, 2 * side + half, i] for i in range(5)]
            for tracer in range(TRACERS):
                at = side * PARTS + 2 * tracer + half
                here = now[row, at]
                value = weights[0] * here + weights[1] * pltpu.roll(here, 1, 1)
                value = value + weights[2] * pltpu.roll(here, 127, 1)
                value = value + weights[3] * now[row - 1, at] + weights[4] * now[row + 1, at]
                done(at, value)


def adjoint_row(now, coefs, row, done):
    for side in range(2):
        for half in range(2):
            which = 2 * side + half
            weights = [coefs[row, which, i] for i in range(3)]
            above = coefs[row + 1, which, 3]
            below = coefs[row - 1, which, 4]
            for tracer in range(TRACERS):
                at = side * PARTS + 2 * tracer + half
                here = now[row, at]
                value = weights[0] * here + pltpu.roll(weights[1] * here, 127, 1)
                value = value + pltpu.roll(weights[2] * here, 1, 1)
                value = value + above * now[row + 1, at] + below * now[row - 1, at]
                done(at, value)


def tangent_kernel(
    inside, inc, wind, south, north, west, east, jac_t, weight, state, changed, wide_wind, now, later, coefs
):
    def setup(row, parts, mask):
        wide = []
        for part in range(PARTS + WINDS):
            found = parts(part)
            left, right = windows(found, part, west[row], east[row])
            if part < PARTS:
                now[row, part] = left * mask
                now[row, PARTS + part] = right * mask
            else:
                wide_wind[row, 2 * (part - PARTS)] = left
                wide_wind[row, 2 * (part - PARTS) + 1] = right
                wide.append((left, right))
        put_coefs(coefs, row, wide, mask)

    for at in range(STEPS):
        setup(at, lambda part: south[at, part * 8 : part * 8 + 8, :], inside[0])
        setup(ROWS + STEPS + at, lambda part: north[at, part * 8 : part * 8 + 8, :], inside[1])

    def own(row, carry):
        setup(STEPS + row, lambda part: own_part(inc, wind, part, row), jnp.float32(1.0))
        return carry

    lax.fori_loop(0, ROWS, own, 0)
    source, sink = now, later
    for step in range(1, STEPS):

        def advance(row, carry, source=source, sink=sink):
            def done(at, value):
                sink[row, at] = value

            tangent_row(source, coefs, row, done)
            return carry

        lax.fori_loop(step, WIDE - step, advance, 0)
        source, sink = sink, source
    jac = flipped(jac_t[...])
    high, low = two_parts(jac * weight[...])
    product = nn(high, jac_t[...]) + nn(low, jac_t[...])
    high, low = two_parts(product)

    def last(row, carry):
        found = {}

        def done(at, value):
            found[at] = value

        tangent_row(source, coefs, row, done)
        full = jnp.concatenate(
            [joined(found[part], found[PARTS + part]) for part in range(PARTS)], axis=0
        ).astype(BF16)
        state[row - STEPS] = full
        changed[row - STEPS] = nn(high, full) + nn(low, full)
        return carry

    lax.fori_loop(STEPS, WIDE - STEPS, last, 0)


def tangent(inside, inc, wind, south, north, west, east, jac_t, weight):
    whole = pl.BlockSpec(memory_space=pltpu.VMEM)
    return pl.pallas_call(
        tangent_kernel,
        in_specs=[pl.BlockSpec(memory_space=pltpu.SMEM)] + [whole] * 8,
        out_shape=[
            jax.ShapeDtypeStruct((ROWS, FEATS, COLS), BF16),
            jax.ShapeDtypeStruct((ROWS, FEATS, COLS), F32),
            jax.ShapeDtypeStruct((WIDE, 2 * WINDS, 8, 128), F32),
        ],
        scratch_shapes=[
            pltpu.VMEM((WIDE, 2 * PARTS, 8, 128), F32),
            pltpu.VMEM((WIDE, 2 * PARTS, 8, 128), F32),
            pltpu.VMEM((WIDE, 4, 5, 8, 128), F32),
        ],
        compiler_params=params(),
        name="tangent",
    )(inside, inc, wind, south, north, west, east, jac_t, weight)


def slot_cells(got):
    coded = got[:, HALF * 128 :].astype(F32)
    return coded * SPLIT + pltpu.roll(coded, 128 - SPLIT, 1) - 1.0


def cell_hits(cells, slot, row):
    lane = iota((cells.shape[0], 128), 1).astype(F32) + row * 128.0
    return (jnp.broadcast_to(cells[:, slot : slot + 1], lane.shape) == lane).astype(F32).astype(BF16)


def gather_kernel(got, state, send):
    cells = slot_cells(got)
    across = jnp.concatenate([flipped(state[row]).astype(BF16) for row in range(ROWS)], axis=0)
    for slot in range(HALF):
        hits = jnp.concatenate([cell_hits(cells, slot, row) for row in range(ROWS)], axis=1)
        send[:, slot * 128 : slot * 128 + 128] = nn(hits, across).astype(BF16)


def gather(got, state):
    return pl.pallas_call(
        gather_kernel,
        out_shape=jax.ShapeDtypeStruct((got.shape[0], HALF * 128), BF16),
        compiler_params=params(),
        name="gather",
    )(got, state)


def scatter_kernel(got, changed, forcing, low, high):
    cells = slot_cells(got)
    rows = got.shape[0]
    terms = jnp.concatenate(
        [flipped(got[:, slot * 128 : slot * 128 + 128]).astype(BF16) for slot in range(HALF)], axis=1
    )
    terms = jnp.concatenate([terms, jnp.ones((16, HALF * rows), BF16)], axis=0)
    for row in range(0, ROWS, 2):
        hits = jnp.concatenate(
            [
                jnp.concatenate([cell_hits(cells, slot, row + at) for slot in range(HALF)], axis=0)
                for at in range(2)
            ],
            axis=1,
        )
        found = nn(terms, hits)
        for at in range(2):
            cut = found[:, at * 128 : at * 128 + 128]
            full = cut[:FEATS] - cut[FEATS : FEATS + 1] * changed[row + at]
            forcing[row + at] = full
            if row + at < STEPS:
                low[row + at] = full.astype(BF16)
            if row + at >= ROWS - STEPS:
                high[row + at - ROWS + STEPS] = full.astype(BF16)


def scatter(got, changed):
    return pl.pallas_call(
        scatter_kernel,
        out_shape=[
            jax.ShapeDtypeStruct((ROWS, FEATS, COLS), F32),
            jax.ShapeDtypeStruct((STEPS, FEATS, COLS), BF16),
            jax.ShapeDtypeStruct((STEPS, FEATS, COLS), BF16),
        ],
        compiler_params=params(),
        name="scatter",
    )(got, changed)


def forcing_edges_kernel(forcing, south, north, low, high):
    def put(row, full):
        pair = pack_row([full[part * 8 : part * 8 + 8] for part in range(PARTS)])
        low[row] = pair[0].astype(BF16)
        high[row] = pair[1].astype(BF16)

    for at in range(STEPS):
        put(at, south[at].astype(F32))
        put(ROWS + STEPS + at, north[at].astype(F32))

    def body(row, carry):
        put(STEPS + row, forcing[row])
        return carry

    lax.fori_loop(0, ROWS, body, 0)


def forcing_edges(forcing, south, north):
    shape = jax.ShapeDtypeStruct((WIDE, 8, 128), BF16)
    return pl.pallas_call(
        forcing_edges_kernel, out_shape=[shape, shape], compiler_params=params(), name="forcing_edges"
    )(forcing, south, north)


def adjoint_kernel(inside, inc, wide_wind, forcing, south, north, west, east, out, now, later, coefs):
    def setup(row, full, mask):
        left_edge = west[row].astype(F32)
        right_edge = east[row].astype(F32)
        for part in range(PARTS):
            found = full[part * 8 : part * 8 + 8]
            now[row, part], now[row, PARTS + part] = windows(found, part, left_edge, right_edge)
        wide = [(wide_wind[row, 2 * at], wide_wind[row, 2 * at + 1]) for at in range(WINDS)]
        put_coefs(coefs, row, wide, mask)

    for at in range(STEPS):
        setup(at, south[at].astype(F32), inside[0])
        setup(ROWS + STEPS + at, north[at].astype(F32), inside[1])

    def own(row, carry):
        setup(STEPS + row, forcing[row], jnp.float32(1.0))
        return carry

    lax.fori_loop(0, ROWS, own, 0)
    source, sink = now, later
    for step in range(1, STEPS):

        def advance(row, carry, source=source, sink=sink):
            def done(at, value):
                sink[row, at] = value

            adjoint_row(source, coefs, row, done)
            return carry

        lax.fori_loop(step, WIDE - step, advance, 0)
        source, sink = sink, source

    def last(row, carry):
        found = {}

        def done(at, value):
            found[at] = value

        adjoint_row(source, coefs, row, done)
        for part in range(PARTS):
            place = pl.ds(part * 8 * ROWS + row - STEPS, 8, stride=ROWS)
            out[place, :] = inc[place, :] - joined(found[part], found[PARTS + part])
        return carry

    lax.fori_loop(STEPS, WIDE - STEPS, last, 0)


def adjoint(inside, inc, wide_wind, forcing, south, north, west, east):
    whole = pl.BlockSpec(memory_space=pltpu.VMEM)
    return pl.pallas_call(
        adjoint_kernel,
        in_specs=[pl.BlockSpec(memory_space=pltpu.SMEM)] + [whole] * 7,
        out_shape=jax.ShapeDtypeStruct(inc.shape, F32),
        scratch_shapes=[
            pltpu.VMEM((WIDE, 2 * PARTS, 8, 128), F32),
            pltpu.VMEM((WIDE, 2 * PARTS, 8, 128), F32),
            pltpu.VMEM((WIDE, 4, 5, 8, 128), F32),
        ],
        compiler_params=params(),
        name="adjoint",
    )(inside, inc, wide_wind, forcing, south, north, west, east)


def depart_kernel(target, back, scores, jac_t, weight, out):
    tiles = back.shape[0] // 2
    pcs, count = scores.shape
    key, rest = keyed(target[...], ranks(target[...]))
    hits = key_hits(key, tiles)
    column = jnp.zeros((FEATS, count), F32)
    for slot in range(HALF):
        column = column + nn(flipped(back[:, slot * 128 : slot * 128 + 128]).astype(BF16), picked(hits, rest, slot))
    scale = jnp.broadcast_to(weight[...], (128, pcs)).T
    column = column.astype(BF16)
    for at in range(0, count, 128):
        model = nn(jac_t[...], column[:, at : at + 128])
        cut = slice(at, at + 128)
        out[:, cut] = (scale * (scores[:, cut].astype(F32) - model)).astype(BF16)


def depart(target, back, scores, jac_t, weight):
    return pl.pallas_call(
        depart_kernel,
        out_shape=jax.ShapeDtypeStruct(scores.shape, BF16),
        compiler_params=params(),
        name="depart",
    )(target, back, scores, jac_t, weight)


def ring(value, axis, move):
    count = lax.axis_size(axis)
    return lax.ppermute(value, axis, [(i, (i + move) % count) for i in range(count)])


def swapped(value):
    tiles = value.shape[0] // 2
    value = value.reshape(tiles, 2, value.shape[1])
    value = lax.all_to_all(value, ("lat", "lon"), split_axis=0, concat_axis=0, tiled=True)
    return value.reshape(2 * tiles, value.shape[2])


def shards(increment, courant, spectra, components, jacobian, obs_weight, tile_target, tile_cell):
    tiles = lax.axis_size("lat") * lax.axis_size("lon")
    count = spectra.shape[0]
    inc = increment.reshape(FEATS * ROWS, COLS)
    wind = courant.reshape(2 * LEVELS * ROWS, COLS)
    target = tile_target.reshape(1, count)
    cell = tile_cell.reshape(1, count)
    jac_t = jacobian.T
    weight = obs_weight.reshape(1, -1)
    band = lax.axis_index("lat")
    inside = jnp.stack([band > 0, band < lax.axis_size("lat") - 1]).astype(F32)

    scores, send = project(target, cell, components, spectra.T, jac_t, weight, tiles)
    got = swapped(send)

    low, high = lat_edges(inc, wind)
    south = ring(high, "lat", 1)
    north = ring(low, "lat", -1)
    low, high = lon_edges(inc, wind, south, north)
    west = ring(high, "lon", 1)
    east = ring(low, "lon", -1)
    state, changed, wide_wind = tangent(inside, inc, wind, south, north, west, east, jac_t, weight)

    back = swapped(gather(got, state))

    forcing, low, high = scatter(got, changed)
    south = ring(high, "lat", 1)
    north = ring(low, "lat", -1)
    low, high = forcing_edges(forcing, south, north)
    west = ring(high, "lon", 1)
    east = ring(low, "lon", -1)
    gradient = adjoint(inside, inc, wide_wind, forcing, south, north, west, east)

    departures = depart(target, back, scores, jac_t, weight)
    return gradient.reshape(increment.shape), departures.T


def solution(mesh):
    placed = (
        P(None, None, "lat", "lon"),
        P(None, None, "lat", "lon"),
        P(("lat", "lon"), None),
        P(),
        P(),
        P(),
        P(("lat", "lon"), None),
        P(("lat", "lon")),
    )
    return jax.shard_map(
        shards,
        mesh=mesh,
        in_specs=placed,
        out_specs=(P(None, None, "lat", "lon"), P(("lat", "lon"), None)),
        check_vma=False,
    )
```

```python
import functools

import jax
import jax.numpy as jnp
from jax import lax
from jax.experimental import pallas as pl
from jax.experimental.pallas import tpu as pltpu
from jax.sharding import PartitionSpec as P

F32 = jnp.float32
BF16 = jnp.bfloat16
TRACERS, LEVELS, ROWS, COLS = 8, 16, 16, 128
FEATS = TRACERS * LEVELS
STEPS = 4
WIDE = ROWS + 2 * STEPS
CAP = 18
LINES, ACROSS = 8, 3
CELLS = CAP // ACROSS
SPLIT = 64
BLOCK = 1280
EARLY = 2
SEGMENTS = 8
SEG = COLS // SEGMENTS
SEG_WIDE = SEG + 2 * STEPS
GROUPS = WIDE // 4
FIRST = 8
EXT = COLS + 2 * FIRST


def params(mib):
    return pltpu.CompilerParams(vmem_limit_bytes=mib * 1024 * 1024)


def took(us):
    return pl.CostEstimate(flops=int(us * 1.15e9), bytes_accessed=int(us * 1e6), transcendentals=0)


def in_hbm(a):
    return pltpu.with_memory_space_constraint(a, pltpu.HBM)


def nn(a, b):
    return lax.dot_general(a, b, (((1,), (0,)), ((), ())), preferred_element_type=F32)


def nt(a, b):
    return lax.dot_general(a, b, (((1,), (1,)), ((), ())), preferred_element_type=F32)


def iota(shape, dim):
    return lax.broadcasted_iota(jnp.int32, shape, dim)


def flipped(a):
    return a.astype(F32).T


def two_parts(a):
    high = a.astype(BF16)
    return high, (a - high.astype(F32)).astype(BF16)


def ranks(target):
    count = target.shape[1]
    tri = (iota((128, 128), 0) <= iota((128, 128), 1)).astype(F32).astype(BF16)
    carry = jnp.zeros((128, 1), F32)
    found = []
    for at in range(0, count, 128):
        hit = (iota((128, 128), 0) == target[:, at : at + 128]).astype(F32)
        upto = nn(hit.astype(BF16), tri) + carry
        carry = upto[:, 127:128]
        found.append(jnp.sum(hit * upto, axis=0, keepdims=True))
    return (jnp.concatenate(found, axis=1) - 1.0).astype(jnp.int32)


def keyed(target, rank):
    line = rank // ACROSS
    return LINES * target + line, rank - ACROSS * line


def key_hits(key, tiles):
    return (iota((LINES * tiles, key.shape[1]), 0) == key).astype(F32).astype(BF16)


def picked(hits, rest, slot):
    chosen = jnp.broadcast_to((rest == slot).astype(F32), (16, rest.shape[1])).astype(BF16)
    rows, count = hits.shape
    return (hits.reshape(rows // 16, 16, count) * chosen[None]).reshape(rows, count)


def begin_kernel(comps, spec, total):
    found = nn(comps[...], spec[...])

    @pl.when(pl.program_id(0) == 0)
    def _():
        total[...] = found

    @pl.when(pl.program_id(0) > 0)
    def _():
        total[...] += found


def begin(comps, spec_t, steps):
    pcs, count = comps.shape[0], spec_t.shape[1]
    return pl.pallas_call(
        begin_kernel,
        grid=(steps,),
        in_specs=[
            pl.BlockSpec((pcs, BLOCK), lambda i: (0, i)),
            pl.BlockSpec((BLOCK, count), lambda i: (i, 0)),
        ],
        out_specs=pl.BlockSpec((pcs, count), lambda i: (0, 0)),
        out_shape=jax.ShapeDtypeStruct((pcs, count), F32),
        compiler_params=params(20), cost_estimate=took(4.5),
        name="begin",
    )(in_hbm(comps), in_hbm(spec_t))


def project_kernel(channels, done, target, cell, comps, spec, total, jac_t, weight, scores, send, sums):
    step = pl.program_id(0)
    steps = pl.num_programs(0)
    count = target.shape[1]
    tiles = send.shape[0] // LINES
    rest = channels - (pl.cdiv(channels, BLOCK) - 1) * BLOCK

    @pl.when(step == 0)
    def _():
        sums[...] = total[...] + nn(comps[...], spec[...])

    @pl.when(jnp.logical_and(step > 0, step < steps - 1))
    def _():
        sums[...] += nn(comps[...], spec[...])

    @pl.when(step == steps - 1)
    def _():
        found = (sums[...] + nn(comps[:, :rest], spec[:rest, :])).astype(BF16)
        scores[...] = found
        high, low = two_parts(flipped(jac_t[...]) * weight[...])
        values = (nn(high, found) + nn(low, found)).T.astype(BF16)
        rank = ranks(target[...])
        key, line = keyed(target[...], rank)
        hits = key_hits(key, tiles)
        for slot in range(1, ACROSS):
            send[:, slot * 128 : slot * 128 + 128] = nn(picked(hits, line, slot), values).astype(BF16)
        number = cell[...] + 1
        upper = number // SPLIT
        lower = number - upper * SPLIT
        lane = iota((128, count), 0)
        coded = jnp.where(lane == rank, upper, 0) + jnp.where(lane - SPLIT == rank, lower, 0)
        here = (iota((tiles, count), 0) == target[...]).astype(F32).astype(BF16)
        codes = nt(here, coded.astype(F32).astype(BF16)).astype(BF16)
        shape = (LINES * tiles, tiles)
        place = (iota(shape, 0) == LINES * iota(shape, 1) + CELLS).astype(F32).astype(BF16)
        send[:, :128] = (nn(picked(hits, line, 0), values) + nn(place, codes)).astype(BF16)


def project(target, cell, comps, spec_t, total, done, jac_t, weight, tiles):
    pcs, channels = comps.shape
    count = spec_t.shape[1]
    steps = pl.cdiv(channels, BLOCK) - done
    whole = lambda a: pl.BlockSpec(a.shape, lambda i: (0, 0))
    return pl.pallas_call(
        functools.partial(project_kernel, channels, done),
        grid=(steps,),
        in_specs=[
            whole(target),
            whole(cell),
            pl.BlockSpec((pcs, BLOCK), lambda i: (0, i + done)),
            pl.BlockSpec((BLOCK, count), lambda i: (i + done, 0)),
            whole(total),
            whole(jac_t),
            whole(weight),
        ],
        out_specs=[
            pl.BlockSpec((pcs, count), lambda i: (0, 0)),
            pl.BlockSpec((LINES * tiles, ACROSS * 128), lambda i: (0, 0)),
        ],
        out_shape=[
            jax.ShapeDtypeStruct((pcs, count), BF16),
            jax.ShapeDtypeStruct((LINES * tiles, ACROSS * 128), BF16),
        ],
        scratch_shapes=[pltpu.VMEM((pcs, count), F32)],
        compiler_params=params(20), cost_estimate=took(13),
        name="project",
    )(target, cell, in_hbm(comps), in_hbm(spec_t), total, jac_t, weight)


def strided(ref, first, count):
    return jnp.concatenate(
        [ref[pl.ds(first + at * ROWS, 8, stride=ROWS), :] for at in range(0, count, 8)], axis=0
    )


def lat_edges_kernel(inc, wind, turned, low, high):
    def turn(row, carry):
        turned[row] = strided(inc, row, FEATS).T
        return carry

    lax.fori_loop(0, ROWS, turn, 0)
    for at in range(STEPS):
        low[at, :FEATS] = turned[at]
        high[at, :FEATS] = turned[ROWS - STEPS + at]
        low[at, FEATS:] = strided(wind, at, 2 * LEVELS)
        high[at, FEATS:] = strided(wind, ROWS - STEPS + at, 2 * LEVELS)


def lat_edges(inc, wind):
    edge = jax.ShapeDtypeStruct((STEPS, FEATS + 2 * LEVELS, COLS), F32)
    return pl.pallas_call(
        lat_edges_kernel,
        out_shape=[jax.ShapeDtypeStruct((ROWS, COLS, FEATS), F32), edge, edge],
        compiler_params=params(4), cost_estimate=took(1.7),
        name="lat_edges",
    )(inc, wind)


def lon_edges_kernel(turned, wind, south, north, winds, low, high):
    for group in range(GROUPS):
        if group == 0:
            four = [south[at, FEATS:] for at in range(4)]
        elif group == GROUPS - 1:
            four = [north[at, FEATS:] for at in range(4)]
        else:
            four = [strided(wind, 4 * group - 4 + at, 2 * LEVELS) for at in range(4)]
        winds[group] = jnp.concatenate(four, axis=0).T
    for row in range(WIDE + GROUPS):
        place = slice(4 * row, 4 * row + 4)
        if row >= WIDE:
            low[place], high[place] = winds[row - WIDE, :4], winds[row - WIDE, COLS - 4 :]
        elif row < STEPS:
            low[place], high[place] = south[row, :4], south[row, COLS - 4 : COLS]
        elif row >= WIDE - STEPS:
            at = row - WIDE + STEPS
            low[place], high[place] = north[at, :4], north[at, COLS - 4 : COLS]
        else:
            low[place], high[place] = turned[row - STEPS, :4], turned[row - STEPS, COLS - 4 :]


def lon_edges(turned, wind, south, north):
    edge = jax.ShapeDtypeStruct((4 * (WIDE + GROUPS), 128), F32)
    return pl.pallas_call(
        lon_edges_kernel,
        out_shape=[jax.ShapeDtypeStruct((GROUPS, COLS, 128), F32), edge, edge],
        compiler_params=params(4), cost_estimate=took(0.3),
        name="lon_edges",
    )(turned, wind, south, north)


def spread(ext, row, full, west, east, mask):
    ext[row, FIRST - 4 : FIRST] = west * mask
    ext[row, FIRST : FIRST + COLS] = full * mask
    ext[row, FIRST + COLS : FIRST + COLS + 4] = east * mask


def segment(ext, row, col):
    return ext[row, pl.ds(FIRST - STEPS + col, SEGMENTS, stride=SEG), :]


def put_coefs(coefs, row, along, across, col, inside):
    coefs[row, col, 0] = (1.0 - along * along - across * across) * inside
    coefs[row, col, 1] = 0.5 * along * (1.0 + along)
    coefs[row, col, 2] = -0.5 * along * (1.0 - along)
    coefs[row, col, 3] = 0.5 * across * (1.0 + across)
    coefs[row, col, 4] = -0.5 * across * (1.0 - across)


def tangent_row(read, coefs, row, step, done):
    west, here = read(row, step - 1), read(row, step)
    for col in range(step, SEG_WIDE - step):
        east = read(row, col + 1)
        value = coefs[row, col, 0] * here + coefs[row, col, 1] * west + coefs[row, col, 2] * east
        value = value + coefs[row, col, 3] * read(row - 1, col) + coefs[row, col, 4] * read(row + 1, col)
        done(col, value)
        west, here = here, east


def adjoint_row(read, coefs, row, step, done):
    def parts(col):
        here = read(row, col)
        return tuple(coefs[row, col, i] * here for i in range(3))

    west, here = parts(step - 1), parts(step)
    for col in range(step, SEG_WIDE - step):
        east = parts(col + 1)
        value = here[0] + east[1] + west[2]
        value = value + coefs[row + 1, col, 3] * read(row + 1, col) + coefs[row - 1, col, 4] * read(row - 1, col)
        done(col, value)
        west, here = here, east


def sweep(one_row, ext, coefs, now, later, finish):
    source = lambda row, col: segment(ext, row, col)
    buffers = (now, later)
    for step in range(1, STEPS + 1):
        sink = buffers[step % 2]

        def advance(row, carry, source=source, sink=sink, step=step):
            def keep(col, value):
                sink[row, col] = value

            last = lambda col, value: finish(row, col, value)
            one_row(source, coefs, row, step, last if step == STEPS else keep)
            return carry

        lax.fori_loop(step, WIDE - step, advance, 0)
        source = lambda row, col, sink=sink: sink[row, col]


def weigh_kernel(winds, west, east, coefs, ext, spot):
    band = lax.axis_index("lat")
    inside = [(band > 0).astype(F32), (band < lax.axis_size("lat") - 1).astype(F32)]
    lane = iota((128, 256), 1)
    for group in range(GROUPS):
        edge = slice(4 * (WIDE + group), 4 * (WIDE + group) + 4)
        spread(spot, 0, winds[group], west[edge], east[edge], 1.0)
        high, low = two_parts(spot[0])
        mask = inside[0] if group == 0 else inside[1] if group == GROUPS - 1 else 1.0
        for at in range(4):
            row = 4 * group + at
            source = 32 * at + LEVELS * (lane // 128) + lane % LEVELS
            copy = (iota((128, 256), 0) == source).astype(F32).astype(BF16)
            both = (nn(high, copy) + nn(low, copy)) * mask
            ext[0, row], ext[1, row] = both[:, :128], both[:, 128:]

    def weigh(row, carry):
        mask = jnp.where(row < STEPS, inside[0], jnp.where(row >= WIDE - STEPS, inside[1], 1.0))
        for col in range(SEG_WIDE):
            along, across = segment(ext.at[0], row, col), segment(ext.at[1], row, col)
            put_coefs(coefs, row, along, across, col, mask)
        return carry

    lax.fori_loop(0, WIDE, weigh, 0)


def weigh(winds, west, east):
    return pl.pallas_call(
        weigh_kernel,
        out_shape=jax.ShapeDtypeStruct((WIDE, SEG_WIDE, 5, 8, 128), F32),
        scratch_shapes=[pltpu.VMEM((2, WIDE, EXT, 128), F32), pltpu.VMEM((1, EXT, 128), F32)],
        compiler_params=params(6), cost_estimate=took(3.3),
        name="weigh",
    )(winds, west, east)


def tangent_kernel(turned, south, north, west, east, coefs, jac_t, weight, state, changed, ext, now, later):
    band = lax.axis_index("lat")
    inside = [(band > 0).astype(F32), (band < lax.axis_size("lat") - 1).astype(F32)]
    for row in range(WIDE):
        edge = slice(4 * row, 4 * row + 4)
        if row < STEPS:
            spread(ext, row, south[row, :FEATS], west[edge], east[edge], inside[0])
        elif row >= WIDE - STEPS:
            spread(ext, row, north[row - WIDE + STEPS, :FEATS], west[edge], east[edge], inside[1])
        else:
            spread(ext, row, turned[row - STEPS], west[edge], east[edge], 1.0)

    def finish(row, col, value):
        changed[row - STEPS, pl.ds(col - STEPS, SEGMENTS, stride=SEG), :] = value

    sweep(tangent_row, ext, coefs, now, later, finish)
    high, low = two_parts(flipped(jac_t[...]) * weight[...])
    high, low = two_parts(nn(high, jac_t[...]) + nn(low, jac_t[...]))
    for row in range(ROWS):
        full = changed[row].astype(BF16)
        state[row] = full
        changed[row] = nn(full, high) + nn(full, low)


def tangent(turned, south, north, west, east, coefs, jac_t, weight):
    return pl.pallas_call(
        tangent_kernel,
        out_shape=[
            jax.ShapeDtypeStruct((ROWS, COLS, FEATS), BF16),
            jax.ShapeDtypeStruct((ROWS, COLS, FEATS), F32),
        ],
        scratch_shapes=[
            pltpu.VMEM((WIDE, EXT, 128), F32),
            pltpu.VMEM((WIDE, SEG_WIDE, 8, 128), F32),
            pltpu.VMEM((WIDE, SEG_WIDE, 8, 128), F32),
        ],
        compiler_params=params(10), cost_estimate=took(4.8),
        name="tangent",
    )(turned, south, north, west, east, coefs, jac_t, weight)


def slot_codes(got, slot):
    rows = got.shape[0]
    coded = got[:, :128].astype(F32).reshape(rows // LINES, LINES, 128)[:, CELLS : CELLS + 1]
    coded = jnp.broadcast_to(coded, (rows // LINES, LINES, 128)).reshape(rows, 128)
    lane = iota((rows, 128), 1) % SPLIT
    return jnp.where(lane == iota((rows, 128), 0) % LINES * ACROSS + slot, coded, 0.0).astype(BF16)


def code_weights(shape, dim):
    return jnp.where(iota(shape, dim) < SPLIT, float(SPLIT), 1.0).astype(BF16)


def place_of(cells):
    upper = jnp.floor(cells * (1.0 / COLS))
    return upper, cells - upper * COLS


def gather_kernel(got, state, send):
    rows = got.shape[0]
    field = state[...].reshape(ROWS * COLS, FEATS)
    lane = iota((rows, 128), 1).astype(F32)
    none = jnp.zeros((rows, 128), BF16)
    for slot in range(ACROSS):
        cells = nn(slot_codes(got, slot), code_weights((128, 128), 0)) - 1.0
        upper, column = place_of(cells)
        upper = upper.astype(BF16)
        along = (column == lane).astype(F32).astype(BF16)
        hits = jnp.concatenate([jnp.where(upper == jnp.bfloat16(row), along, none) for row in range(ROWS)], axis=1)
        send[:, slot * 128 : slot * 128 + 128] = nn(hits, field).astype(BF16)


def gather(got, state):
    return pl.pallas_call(
        gather_kernel,
        out_shape=jax.ShapeDtypeStruct(got.shape, BF16),
        compiler_params=params(10), cost_estimate=took(3.9),
        name="gather",
    )(got, state)


def scatter_kernel(got, changed, forcing, low, high):
    rows = got.shape[0]
    cells = jnp.concatenate(
        [nt(code_weights((16, 128), 1), slot_codes(got, slot))[:1] - 1.0 for slot in range(ACROSS)], axis=1
    )
    terms = jnp.concatenate([got[:, slot * 128 : slot * 128 + 128] for slot in range(ACROSS)], axis=0)
    terms = jnp.concatenate([terms, jnp.ones(terms.shape, BF16)], axis=1)
    shape = (COLS, ACROSS * rows)
    upper, column = place_of(cells)
    along = (iota(shape, 0).astype(F32) == column).astype(F32).astype(BF16)
    upper = jnp.broadcast_to(upper, shape).astype(BF16)
    none = jnp.zeros(shape, BF16)
    for row in range(ROWS):
        found = nn(jnp.where(upper == jnp.bfloat16(row), along, none), terms)
        full = found[:, :FEATS] - found[:, FEATS:] * changed[row]
        forcing[row] = full
        if row < STEPS:
            low[row] = full.astype(BF16)
        if row >= ROWS - STEPS:
            high[row - ROWS + STEPS] = full.astype(BF16)


def scatter(got, changed):
    edge = jax.ShapeDtypeStruct((STEPS, COLS, FEATS), BF16)
    return pl.pallas_call(
        scatter_kernel,
        out_shape=[jax.ShapeDtypeStruct((ROWS, COLS, FEATS), F32), edge, edge],
        compiler_params=params(10), cost_estimate=took(3.7),
        name="scatter",
    )(got, changed)


def forcing_edges_kernel(forcing, south, north, low, high):
    first, last = [], []
    for row in range(WIDE):
        if row < STEPS:
            full = south[row].astype(F32)
        elif row >= WIDE - STEPS:
            full = north[row - WIDE + STEPS].astype(F32)
        else:
            full = forcing[row - STEPS]
        first.append(full[:4])
        last.append(full[COLS - 4 :])
    low[...] = jnp.concatenate(first, axis=0).astype(BF16)
    high[...] = jnp.concatenate(last, axis=0).astype(BF16)


def forcing_edges(forcing, south, north):
    edge = jax.ShapeDtypeStruct((4 * WIDE, FEATS), BF16)
    return pl.pallas_call(
        forcing_edges_kernel, out_shape=[edge, edge], compiler_params=params(4), cost_estimate=took(0.3), name="forcing_edges"
    )(forcing, south, north)


def adjoint_kernel(inc, coefs, forcing, south, north, west, east, out, ext, back, now, later):
    left, right = west[...].astype(F32), east[...].astype(F32)
    for row in range(WIDE):
        if row < STEPS:
            full = south[row].astype(F32)
        elif row >= WIDE - STEPS:
            full = north[row - WIDE + STEPS].astype(F32)
        else:
            full = forcing[row - STEPS]
        edge = slice(4 * row, 4 * row + 4)
        spread(ext, row, full, left[edge], right[edge], 1.0)

    def finish(row, col, value):
        back[row - STEPS, pl.ds(col - STEPS, SEGMENTS, stride=SEG), :] = value

    sweep(adjoint_row, ext, coefs, now, later, finish)

    def turn(row, carry):
        full = back[row].T
        for at in range(0, FEATS, 8):
            place = pl.ds(at * ROWS + row, 8, stride=ROWS)
            out[place, :] = inc[place, :] - full[at : at + 8]
        return carry

    lax.fori_loop(0, ROWS, turn, 0)


def adjoint(inc, coefs, forcing, south, north, west, east):
    return pl.pallas_call(
        adjoint_kernel,
        out_shape=jax.ShapeDtypeStruct(inc.shape, F32),
        scratch_shapes=[
            pltpu.VMEM((WIDE, EXT, 128), F32),
            pltpu.VMEM((ROWS, COLS, FEATS), F32),
            pltpu.VMEM((WIDE, SEG_WIDE, 8, 128), F32),
            pltpu.VMEM((WIDE, SEG_WIDE, 8, 128), F32),
        ],
        compiler_params=params(10), cost_estimate=took(7),
        name="adjoint",
    )(inc, coefs, forcing, south, north, west, east)


def depart_kernel(target, back, scores, jac_t, weight, out):
    tiles = back.shape[0] // LINES
    pcs, count = scores.shape
    key, rest = keyed(target[...], ranks(target[...]))
    hits = key_hits(key, tiles)
    column = jnp.zeros((FEATS, count), F32)
    for slot in range(ACROSS):
        mine = flipped(back[:, slot * 128 : slot * 128 + 128]).astype(BF16)
        column = column + nn(mine, picked(hits, rest, slot))
    scale = jnp.broadcast_to(weight[...], (128, pcs)).T
    column = column.astype(BF16)
    for at in range(0, count, 128):
        model = nn(jac_t[...], column[:, at : at + 128])
        cut = slice(at, at + 128)
        out[:, cut] = (scale * (scores[:, cut].astype(F32) - model)).astype(BF16)


def depart(target, back, scores, jac_t, weight):
    return pl.pallas_call(
        depart_kernel,
        out_shape=jax.ShapeDtypeStruct(scores.shape, BF16),
        compiler_params=params(10), cost_estimate=took(3.5),
        name="depart",
    )(target, back, scores, jac_t, weight)


def ring(value, axis, move):
    count = lax.axis_size(axis)
    return lax.ppermute(value, axis, [(i, (i + move) % count) for i in range(count)])


def swapped(value):
    tiles = value.shape[0] // LINES
    value = value.reshape(tiles, LINES, value.shape[1])
    value = lax.all_to_all(value, ("lat", "lon"), split_axis=0, concat_axis=0, tiled=True)
    return value.reshape(LINES * tiles, value.shape[2])


def shards(increment, courant, spectra, components, jacobian, obs_weight, tile_target, tile_cell):
    tiles = lax.axis_size("lat") * lax.axis_size("lon")
    count = spectra.shape[0]
    inc = increment.reshape(FEATS * ROWS, COLS)
    wind = courant.reshape(2 * LEVELS * ROWS, COLS)
    target = tile_target.reshape(1, count)
    cell = tile_cell.reshape(1, count)
    jac_t = jacobian.T
    weight = obs_weight.reshape(1, -1)

    turned, low, high = lat_edges(inc, wind)
    south = ring(high, "lat", 1)
    north = ring(low, "lat", -1)
    total = begin(components, spectra.T, EARLY)
    total, south, north = lax.optimization_barrier((total, south, north))
    winds, low, high = lon_edges(turned, wind, south, north)
    west = ring(high, "lon", 1)
    east = ring(low, "lon", -1)
    scores, send = project(target, cell, components, spectra.T, total, EARLY, jac_t, weight, tiles)
    send, west, east = lax.optimization_barrier((send, west, east))
    got = swapped(send)
    coefs = weigh(winds, west, east)
    state, changed = tangent(turned, south, north, west, east, coefs, jac_t, weight)

    send = gather(got, state)
    forcing, low, high = scatter(got, changed)
    south = ring(high, "lat", 1)
    north = ring(low, "lat", -1)
    send, forcing = lax.optimization_barrier((send, forcing))
    back = swapped(send)
    low, winds = lax.optimization_barrier((low, winds))
    coefs = weigh(winds, west, east)
    low, high = forcing_edges(forcing, south, north)
    west = ring(high, "lon", 1)
    east = ring(low, "lon", -1)
    gradient = adjoint(inc, coefs, forcing, south, north, west, east)

    departures = depart(target, back, scores, jac_t, weight)
    return gradient.reshape(increment.shape), departures.T


def solution(mesh):
    placed = (
        P(None, None, "lat", "lon"),
        P(None, None, "lat", "lon"),
        P(("lat", "lon"), None),
        P(),
        P(),
        P(),
        P(("lat", "lon"), None),
        P(("lat", "lon")),
    )
    return jax.shard_map(
        shards,
        mesh=mesh,
        in_specs=placed,
        out_specs=(P(None, None, "lat", "lon"), P(("lat", "lon"), None)),
        check_vma=False,
    )
```

```python
import functools

import jax
import jax.numpy as jnp
from jax import lax
from jax.experimental import pallas as pl
from jax.experimental.pallas import tpu as pltpu
from jax.sharding import PartitionSpec as P

F32 = jnp.float32
BF16 = jnp.bfloat16
TRACERS, LEVELS, ROWS, COLS = 8, 16, 16, 128
FEATS = TRACERS * LEVELS
STEPS = 4
WIDE = ROWS + 2 * STEPS
CAP = 18
LINES, ACROSS = 4, 5
CELL_LINE, CELL_SLOT = CAP // ACROSS, CAP % ACROSS
SPLIT = 64
BLOCK = 1280
EARLY = 2
MANY = 4
SEGMENTS = 8
SEG = COLS // SEGMENTS
SEG_WIDE = SEG + 2 * STEPS
GROUPS = WIDE // 4
FIRST = 8
EXT = COLS + 2 * FIRST


def params(mib):
    return pltpu.CompilerParams(vmem_limit_bytes=mib * 1024 * 1024)


def took(us):
    return pl.CostEstimate(flops=int(us * 1.15e9), bytes_accessed=int(us * 1e6), transcendentals=0)


def in_hbm(a):
    return pltpu.with_memory_space_constraint(a, pltpu.HBM)


def nn(a, b):
    return lax.dot_general(a, b, (((1,), (0,)), ((), ())), preferred_element_type=F32)


def nt(a, b):
    return lax.dot_general(a, b, (((1,), (1,)), ((), ())), preferred_element_type=F32)


def iota(shape, dim):
    return lax.broadcasted_iota(jnp.int32, shape, dim)


def flipped(a):
    return a.astype(F32).T


def two_parts(a):
    high = a.astype(BF16)
    return high, (a - high.astype(F32)).astype(BF16)


def ranks(target):
    count = target.shape[1]
    tri = (iota((128, 128), 0) <= iota((128, 128), 1)).astype(F32).astype(BF16)
    carry = jnp.zeros((128, 1), F32)
    found = []
    for at in range(0, count, 128):
        hit = (iota((128, 128), 0) == target[:, at : at + 128]).astype(F32)
        upto = nn(hit.astype(BF16), tri) + carry
        carry = upto[:, 127:128]
        found.append(jnp.sum(hit * upto, axis=0, keepdims=True))
    return (jnp.concatenate(found, axis=1) - 1.0).astype(jnp.int32)


def keyed(target, rank):
    line = rank // ACROSS
    return LINES * target + line, rank - ACROSS * line


def key_hits(key, tiles):
    return (iota((LINES * tiles, key.shape[1]), 0) == key).astype(F32).astype(BF16)


def begin_kernel(comps, spec, total):
    found = nn(comps[...], spec[...])

    @pl.when(pl.program_id(0) == 0)
    def _():
        total[...] = found

    @pl.when(pl.program_id(0) > 0)
    def _():
        total[...] += found


def begin(comps, spec_t, steps):
    pcs, count = comps.shape[0], spec_t.shape[1]
    return pl.pallas_call(
        begin_kernel,
        grid=(steps,),
        in_specs=[
            pl.BlockSpec((pcs, BLOCK), lambda i: (0, i)),
            pl.BlockSpec((BLOCK, count), lambda i: (i, 0)),
        ],
        out_specs=pl.BlockSpec((pcs, count), lambda i: (0, 0)),
        out_shape=jax.ShapeDtypeStruct((pcs, count), F32),
        compiler_params=params(20), cost_estimate=took(4.5),
        name="begin",
    )(in_hbm(comps), in_hbm(spec_t))


def project_kernel(channels, done, target, cell, comps, spec, total, jac_t, weight, scores, send, sums):
    step = pl.program_id(0)
    steps = pl.num_programs(0)
    count = target.shape[1]
    tiles = send.shape[0]
    rest = channels - (pl.cdiv(channels, BLOCK) - 1) * BLOCK

    @pl.when(step == 0)
    def _():
        sums[...] = total[...] + nn(comps[...], spec[...])

    @pl.when(jnp.logical_and(step > 0, step < steps - 1))
    def _():
        sums[...] += nn(comps[...], spec[...])

    @pl.when(step == steps - 1)
    def _():
        found = (sums[...] + nn(comps[:, :rest], spec[:rest, :])).astype(BF16)
        scores[...] = found
        high, low = two_parts(flipped(jac_t[...]) * weight[...].reshape(1, -1))
        values = nn(high, found) + nn(low, found)
        rank = ranks(target[...])
        key, line = keyed(target[...], rank)
        values = jnp.concatenate([jnp.where(line == slot, values, 0.0) for slot in range(ACROSS)], axis=0)
        packed = nn(key_hits(key, tiles), values.T.astype(BF16))
        number = cell[...].reshape(1, count) + 1
        upper = number // SPLIT
        lower = number - upper * SPLIT
        lane = iota((128, count), 0)
        coded = jnp.where(lane == rank, upper, 0) + jnp.where(lane - SPLIT == rank, lower, 0)
        here = (iota((tiles, count), 0) == target[...]).astype(F32).astype(BF16)
        codes = nt(here, coded.astype(F32).astype(BF16)).astype(BF16)
        shape = (LINES * tiles, tiles)
        place = (iota(shape, 0) == LINES * iota(shape, 1) + CELL_LINE).astype(F32).astype(BF16)
        codes = nn(place, codes)
        for slot in range(ACROSS):
            cut = slice(slot * 128, slot * 128 + 128)
            full = packed[:, cut] + codes if slot == CELL_SLOT else packed[:, cut]
            send[:, :, cut] = full.astype(BF16).reshape(tiles, LINES, 128)


def project(target, cell, comps, spec_t, total, done, jac_t, weight, tiles):
    pcs, channels = comps.shape
    count = spec_t.shape[1]
    steps = pl.cdiv(channels, BLOCK) - done
    whole = lambda a: pl.BlockSpec(a.shape, lambda i: (0,) * a.ndim)
    return pl.pallas_call(
        functools.partial(project_kernel, channels, done),
        grid=(steps,),
        in_specs=[
            whole(target),
            whole(cell),
            pl.BlockSpec((pcs, BLOCK), lambda i: (0, i + done)),
            pl.BlockSpec((BLOCK, count), lambda i: (i + done, 0)),
            whole(total),
            whole(jac_t),
            whole(weight),
        ],
        out_specs=[
            pl.BlockSpec((pcs, count), lambda i: (0, 0)),
            pl.BlockSpec((tiles, LINES, ACROSS * 128), lambda i: (0, 0, 0)),
        ],
        out_shape=[
            jax.ShapeDtypeStruct((pcs, count), BF16),
            jax.ShapeDtypeStruct((tiles, LINES, ACROSS * 128), BF16),
        ],
        scratch_shapes=[pltpu.VMEM((pcs, count), F32)],
        compiler_params=params(20), cost_estimate=took(13),
        name="project",
    )(target, cell, in_hbm(comps), in_hbm(spec_t), total, jac_t, weight)


def strided(ref, first, count):
    return jnp.concatenate(
        [ref[pl.ds(first + at * ROWS, 8, stride=ROWS), :] for at in range(0, count, 8)], axis=0
    )


def lat_edges_kernel(inc, wind, turned, low, high):
    def turn(row, carry):
        turned[row] = strided(inc, row, FEATS).T
        return carry

    lax.fori_loop(0, ROWS, turn, 0)
    for at in range(STEPS):
        low[at, :FEATS] = turned[at]
        high[at, :FEATS] = turned[ROWS - STEPS + at]
        low[at, FEATS:] = strided(wind, at, 2 * LEVELS)
        high[at, FEATS:] = strided(wind, ROWS - STEPS + at, 2 * LEVELS)


def lat_edges(inc, wind):
    edge = jax.ShapeDtypeStruct((STEPS, FEATS + 2 * LEVELS, COLS), F32)
    return pl.pallas_call(
        lat_edges_kernel,
        out_shape=[jax.ShapeDtypeStruct((ROWS, COLS, FEATS), F32), edge, edge],
        compiler_params=params(6), cost_estimate=took(1.7),
        name="lat_edges",
    )(in_hbm(inc), in_hbm(wind))


def lon_edges_kernel(turned, wind, south, north, winds, low, high):
    for group in range(GROUPS):
        if group == 0:
            four = [south[at, FEATS:] for at in range(4)]
        elif group == GROUPS - 1:
            four = [north[at, FEATS:] for at in range(4)]
        else:
            four = [strided(wind, 4 * group - 4 + at, 2 * LEVELS) for at in range(4)]
        winds[group] = jnp.concatenate(four, axis=0).T
    for row in range(WIDE + GROUPS):
        place = slice(4 * row, 4 * row + 4)
        if row >= WIDE:
            low[place], high[place] = winds[row - WIDE, :4], winds[row - WIDE, COLS - 4 :]
        elif row < STEPS:
            low[place], high[place] = south[row, :4], south[row, COLS - 4 : COLS]
        elif row >= WIDE - STEPS:
            at = row - WIDE + STEPS
            low[place], high[place] = north[at, :4], north[at, COLS - 4 : COLS]
        else:
            low[place], high[place] = turned[row - STEPS, :4], turned[row - STEPS, COLS - 4 :]


def lon_edges(turned, wind, south, north):
    edge = jax.ShapeDtypeStruct((4 * (WIDE + GROUPS), 128), F32)
    return pl.pallas_call(
        lon_edges_kernel,
        out_shape=[jax.ShapeDtypeStruct((GROUPS, COLS, 128), F32), edge, edge],
        compiler_params=params(4), cost_estimate=took(0.3),
        name="lon_edges",
    )(turned, wind, south, north)


def spread(ext, row, full, west, east, mask):
    ext[row, FIRST - 4 : FIRST] = west * mask
    ext[row, FIRST : FIRST + COLS] = full * mask
    ext[row, FIRST + COLS : FIRST + COLS + 4] = east * mask


def segment(ext, row, col):
    return ext[row, pl.ds(FIRST - STEPS + col, SEGMENTS, stride=SEG), :]


def put_coefs(coefs, row, along, across, col, inside):
    coefs[row, col, 0] = (1.0 - along * along - across * across) * inside
    coefs[row, col, 1] = 0.5 * along * (1.0 + along)
    coefs[row, col, 2] = -0.5 * along * (1.0 - along)
    coefs[row, col, 3] = 0.5 * across * (1.0 + across)
    coefs[row, col, 4] = -0.5 * across * (1.0 - across)


def tangent_row(read, coefs, row, step, done):
    west, here = read(row, step - 1), read(row, step)
    for col in range(step, SEG_WIDE - step):
        east = read(row, col + 1)
        value = coefs[row, col, 0] * here + coefs[row, col, 1] * west + coefs[row, col, 2] * east
        value = value + coefs[row, col, 3] * read(row - 1, col) + coefs[row, col, 4] * read(row + 1, col)
        done(col, value)
        west, here = here, east


def adjoint_row(read, coefs, row, step, done):
    def parts(col):
        here = read(row, col)
        return tuple(coefs[row, col, i] * here for i in range(3))

    west, here = parts(step - 1), parts(step)
    for col in range(step, SEG_WIDE - step):
        east = parts(col + 1)
        value = here[0] + east[1] + west[2]
        value = value + coefs[row + 1, col, 3] * read(row + 1, col) + coefs[row - 1, col, 4] * read(row - 1, col)
        done(col, value)
        west, here = here, east


def sweep(one_row, ext, coefs, now, later, finish):
    source = lambda row, col: segment(ext, row, col)
    buffers = (now, later)
    for step in range(1, STEPS + 1):
        sink = buffers[step % 2]

        def advance(row, carry, source=source, sink=sink, step=step):
            def keep(col, value):
                sink[row, col] = value

            last = lambda col, value: finish(row, col, value)
            one_row(source, coefs, row, step, last if step == STEPS else keep)
            return carry

        lax.fori_loop(step, WIDE - step, advance, 0)
        source = lambda row, col, sink=sink: sink[row, col]


def weigh_kernel(winds, west, east, coefs, ext, spot):
    band = lax.axis_index("lat")
    inside = [(band > 0).astype(F32), (band < lax.axis_size("lat") - 1).astype(F32)]
    lane = iota((128, 256), 1)
    for group in range(GROUPS):
        edge = slice(4 * (WIDE + group), 4 * (WIDE + group) + 4)
        spread(spot, 0, winds[group], west[edge], east[edge], 1.0)
        high, low = two_parts(spot[0])
        mask = inside[0] if group == 0 else inside[1] if group == GROUPS - 1 else 1.0
        for at in range(4):
            row = 4 * group + at
            source = 32 * at + LEVELS * (lane // 128) + lane % LEVELS
            copy = (iota((128, 256), 0) == source).astype(F32).astype(BF16)
            both = (nn(high, copy) + nn(low, copy)) * mask
            ext[0, row], ext[1, row] = both[:, :128], both[:, 128:]

    def weigh(row, carry):
        mask = jnp.where(row < STEPS, inside[0], jnp.where(row >= WIDE - STEPS, inside[1], 1.0))
        for col in range(SEG_WIDE):
            along, across = segment(ext.at[0], row, col), segment(ext.at[1], row, col)
            put_coefs(coefs, row, along, across, col, mask)
        return carry

    lax.fori_loop(0, WIDE, weigh, 0)


def weigh(winds, west, east):
    return pl.pallas_call(
        weigh_kernel,
        out_shape=jax.ShapeDtypeStruct((WIDE, SEG_WIDE, 5, 8, 128), F32),
        scratch_shapes=[pltpu.VMEM((2, WIDE, EXT, 128), F32), pltpu.VMEM((1, EXT, 128), F32)],
        compiler_params=params(6), cost_estimate=took(3.3),
        name="weigh",
    )(winds, west, east)


def tangent_kernel(turned, south, north, west, east, coefs, jac_t, weight, state, changed, ext, now, later):
    band = lax.axis_index("lat")
    inside = [(band > 0).astype(F32), (band < lax.axis_size("lat") - 1).astype(F32)]
    for row in range(WIDE):
        edge = slice(4 * row, 4 * row + 4)
        if row < STEPS:
            spread(ext, row, south[row, :FEATS], west[edge], east[edge], inside[0])
        elif row >= WIDE - STEPS:
            spread(ext, row, north[row - WIDE + STEPS, :FEATS], west[edge], east[edge], inside[1])
        else:
            spread(ext, row, turned[row - STEPS], west[edge], east[edge], 1.0)

    def finish(row, col, value):
        changed[row - STEPS, pl.ds(col - STEPS, SEGMENTS, stride=SEG), :] = value

    sweep(tangent_row, ext, coefs, now, later, finish)
    high, low = two_parts(flipped(jac_t[...]) * weight[...].reshape(1, -1))
    high, low = two_parts(nn(high, jac_t[...]) + nn(low, jac_t[...]))
    for row in range(ROWS):
        full = changed[row].astype(BF16)
        state[row] = full
    state[ROWS], state[ROWS + 1] = high, low


def tangent(turned, south, north, west, east, coefs, jac_t, weight):
    return pl.pallas_call(
        tangent_kernel,
        out_shape=jax.ShapeDtypeStruct((ROWS + 2, COLS, FEATS), BF16),
        scratch_shapes=[
            pltpu.VMEM((ROWS, COLS, FEATS), F32),
            pltpu.VMEM((WIDE, EXT, 128), F32),
            pltpu.VMEM((WIDE, SEG_WIDE, 8, 128), F32),
            pltpu.VMEM((WIDE, SEG_WIDE, 8, 128), F32),
        ],
        compiler_params=params(10), cost_estimate=took(4.8),
        name="tangent",
    )(turned, south, north, west, east, coefs, jac_t, weight)


def slot_of(message, slot):
    cut = message[:, :, slot * 128 : slot * 128 + 128]
    return cut.reshape(cut.shape[0] * LINES, 128)


def slot_codes(got, slot):
    rows = got.shape[0] * LINES
    coded = slot_of(got, CELL_SLOT).astype(F32).reshape(got.shape[0], LINES, 128)[:, CELL_LINE : CELL_LINE + 1]
    coded = jnp.broadcast_to(coded, (got.shape[0], LINES, 128)).reshape(rows, 128)
    lane = iota((rows, 128), 1) % SPLIT
    return jnp.where(lane == iota((rows, 128), 0) % LINES * ACROSS + slot, coded, 0.0).astype(BF16)


def code_weights(shape, dim):
    return jnp.where(iota(shape, dim) < SPLIT, float(SPLIT), 1.0).astype(BF16)


def place_of(cells):
    upper = jnp.floor(cells * (1.0 / COLS))
    return upper, cells - upper * COLS


def gather_kernel(got, state, send):
    rows = got.shape[0] * LINES
    field = state[:ROWS].reshape(ROWS * COLS, FEATS)
    lane = iota((rows, 128), 1).astype(F32)
    none = jnp.zeros((rows, 128), BF16)
    for slot in range(ACROSS):
        cells = nn(slot_codes(got, slot), code_weights((128, 128), 0)) - 1.0
        upper, column = place_of(cells)
        upper = upper.astype(BF16)
        along = (column == lane).astype(F32).astype(BF16)
        hits = jnp.concatenate([jnp.where(upper == jnp.bfloat16(row), along, none) for row in range(ROWS)], axis=1)
        found = nn(hits, field).astype(BF16)
        send[:, :, slot * 128 : slot * 128 + 128] = found.reshape(got.shape[0], LINES, 128)


def gather(got, state):
    return pl.pallas_call(
        gather_kernel,
        out_shape=jax.ShapeDtypeStruct(got.shape, BF16),
        compiler_params=params(10), cost_estimate=took(3.9),
        name="gather",
    )(got, state)


def scatter_kernel(got, state, forcing, low, high):
    rows = got.shape[0] * LINES
    cells = jnp.concatenate(
        [nt(code_weights((16, 128), 1), slot_codes(got, slot))[:1] - 1.0 for slot in range(ACROSS)], axis=1
    )
    terms = jnp.concatenate([slot_of(got, slot) for slot in range(ACROSS)], axis=0)
    terms = jnp.concatenate([terms, jnp.ones(terms.shape, BF16)], axis=1)
    shape = (COLS, ACROSS * rows)
    upper, column = place_of(cells)
    along = (iota(shape, 0).astype(F32) == column).astype(F32).astype(BF16)
    upper = jnp.broadcast_to(upper, shape).astype(BF16)
    none = jnp.zeros(shape, BF16)
    change = jnp.concatenate([state[ROWS], state[ROWS + 1]], axis=1)
    for first in range(0, ROWS, MANY):
        hits = [jnp.where(upper == jnp.bfloat16(first + at), along, none) for at in range(MANY)]
        found = nn(jnp.concatenate(hits, axis=0), terms)
        changed = nn(state[first : first + MANY].reshape(MANY * COLS, FEATS), change)
        changed = changed[:, :FEATS] + changed[:, FEATS:]
        full = (found[:, :FEATS] - found[:, FEATS:] * changed).reshape(MANY, COLS, FEATS)
        forcing[first : first + MANY] = full
        if first == 0:
            low[...] = full[:STEPS].astype(BF16)
        if first + MANY == ROWS:
            high[...] = full[MANY - STEPS :].astype(BF16)


def scatter(got, state):
    edge = jax.ShapeDtypeStruct((STEPS, COLS, FEATS), BF16)
    return pl.pallas_call(
        scatter_kernel,
        out_shape=[jax.ShapeDtypeStruct((ROWS, COLS, FEATS), F32), edge, edge],
        compiler_params=params(14), cost_estimate=took(3.7),
        name="scatter",
    )(got, state)


def forcing_edges_kernel(forcing, south, north, low, high):
    first, last = [], []
    for row in range(WIDE):
        if row < STEPS:
            full = south[row].astype(F32)
        elif row >= WIDE - STEPS:
            full = north[row - WIDE + STEPS].astype(F32)
        else:
            full = forcing[row - STEPS]
        first.append(full[:4])
        last.append(full[COLS - 4 :])
    low[...] = jnp.concatenate(first, axis=0).astype(BF16)
    high[...] = jnp.concatenate(last, axis=0).astype(BF16)


def forcing_edges(forcing, south, north):
    edge = jax.ShapeDtypeStruct((4 * WIDE, FEATS), BF16)
    return pl.pallas_call(
        forcing_edges_kernel, out_shape=[edge, edge], compiler_params=params(4), cost_estimate=took(0.3), name="forcing_edges"
    )(forcing, south, north)


def adjoint_kernel(inc, coefs, forcing, south, north, west, east, out, ext, back, now, later):
    left, right = west[...].astype(F32), east[...].astype(F32)
    for row in range(WIDE):
        if row < STEPS:
            full = south[row].astype(F32)
        elif row >= WIDE - STEPS:
            full = north[row - WIDE + STEPS].astype(F32)
        else:
            full = forcing[row - STEPS]
        edge = slice(4 * row, 4 * row + 4)
        spread(ext, row, full, left[edge], right[edge], 1.0)

    def finish(row, col, value):
        back[row - STEPS, pl.ds(col - STEPS, SEGMENTS, stride=SEG), :] = value

    sweep(adjoint_row, ext, coefs, now, later, finish)

    def turn(row, carry):
        full = back[row].T
        for at in range(0, FEATS, 8):
            place = pl.ds(at * ROWS + row, 8, stride=ROWS)
            out[place, :] = inc[place, :] - full[at : at + 8]
        return carry

    lax.fori_loop(0, ROWS, turn, 0)


def adjoint(inc, coefs, forcing, south, north, west, east):
    return pl.pallas_call(
        adjoint_kernel,
        out_shape=jax.ShapeDtypeStruct(inc.shape, F32),
        scratch_shapes=[
            pltpu.VMEM((WIDE, EXT, 128), F32),
            pltpu.VMEM((ROWS, COLS, FEATS), F32),
            pltpu.VMEM((WIDE, SEG_WIDE, 8, 128), F32),
            pltpu.VMEM((WIDE, SEG_WIDE, 8, 128), F32),
        ],
        compiler_params=params(10), cost_estimate=took(7),
        name="adjoint",
    )(inc, coefs, forcing, south, north, west, east)


def depart_kernel(target, back, scores, jac_t, weight, out):
    tiles = back.shape[0]
    pcs, count = scores.shape
    key, rest = keyed(target[...], ranks(target[...]))
    sent = jnp.concatenate([flipped(slot_of(back, slot)).astype(BF16) for slot in range(ACROSS)], axis=0)
    found = nn(sent, key_hits(key, tiles))
    column = jnp.zeros((FEATS, count), F32)
    for slot in range(ACROSS):
        column = jnp.where(rest == slot, found[slot * FEATS : (slot + 1) * FEATS], column)
    scale = jnp.broadcast_to(weight[...].reshape(1, -1), (128, pcs)).T
    column = column.astype(BF16)
    for at in range(0, count, 128):
        model = nn(jac_t[...], column[:, at : at + 128])
        cut = slice(at, at + 128)
        out[:, cut] = (scale * (scores[:, cut].astype(F32) - model)).astype(BF16)


def depart(target, back, scores, jac_t, weight):
    return pl.pallas_call(
        depart_kernel,
        out_shape=jax.ShapeDtypeStruct(scores.shape, BF16),
        compiler_params=params(10), cost_estimate=took(3.5),
        name="depart",
    )(target, back, scores, jac_t, weight)


def ring(value, axis, move):
    count = lax.axis_size(axis)
    return lax.ppermute(value, axis, [(i, (i + move) % count) for i in range(count)])


def swapped(value):
    return lax.all_to_all(value, ("lat", "lon"), split_axis=0, concat_axis=0, tiled=True)


def shards(increment, courant, spectra, components, jacobian, obs_weight, tile_target, tile_cell):
    tiles = lax.axis_size("lat") * lax.axis_size("lon")
    count = spectra.shape[0]
    inc = increment.reshape(FEATS * ROWS, COLS)
    wind = courant.reshape(2 * LEVELS * ROWS, COLS)
    target = tile_target.reshape(1, count)
    cell = tile_cell
    jac_t = jacobian.T
    weight = obs_weight

    turned, low, high = lat_edges(inc, wind)
    south = ring(high, "lat", 1)
    north = ring(low, "lat", -1)
    total = begin(components, spectra.T, EARLY)
    total, south, north = lax.optimization_barrier((total, south, north))
    winds, low, high = lon_edges(turned, wind, south, north)
    west = ring(high, "lon", 1)
    east = ring(low, "lon", -1)
    scores, send = project(target, cell, components, spectra.T, total, EARLY, jac_t, weight, tiles)
    send, west, east = lax.optimization_barrier((send, west, east))
    got = swapped(send)
    coefs = weigh(winds, west, east)
    state = tangent(turned, south, north, west, east, coefs, jac_t, weight)

    send = gather(got, state)
    forcing, low, high = scatter(got, state)
    south = ring(high, "lat", 1)
    north = ring(low, "lat", -1)
    send, forcing = lax.optimization_barrier((send, forcing))
    back = swapped(send)
    low, winds = lax.optimization_barrier((low, winds))
    coefs = weigh(winds, west, east)
    low, high = forcing_edges(forcing, south, north)
    west = ring(high, "lon", 1)
    east = ring(low, "lon", -1)
    gradient = adjoint(inc, coefs, forcing, south, north, west, east)

    departures = depart(target, back, scores, jac_t, weight)
    return gradient.reshape(increment.shape), departures.T


def solution(mesh):
    placed = (
        P(None, None, "lat", "lon"),
        P(None, None, "lat", "lon"),
        P(("lat", "lon"), None),
        P(),
        P(),
        P(),
        P(("lat", "lon"), None),
        P(("lat", "lon")),
    )
    return jax.shard_map(
        shards,
        mesh=mesh,
        in_specs=placed,
        out_specs=(P(None, None, "lat", "lon"), P(("lat", "lon"), None)),
        check_vma=False,
    )
```

```python
import functools

import jax
import jax.numpy as jnp
from jax import lax
from jax.experimental import pallas as pl
from jax.experimental.pallas import tpu as pltpu
from jax.sharding import PartitionSpec as P

F32 = jnp.float32
BF16 = jnp.bfloat16
TRACERS, LEVELS, ROWS, COLS = 8, 16, 16, 128
FEATS = TRACERS * LEVELS
STEPS = 4
WIDE = ROWS + 2 * STEPS
CAP = 18
LINES, ACROSS = 4, 5
CELL_LINE, CELL_SLOT = CAP // ACROSS, CAP % ACROSS
SPLIT = 64
BLOCK = 1280
EARLY = 2
MANY = 4
SEGMENTS = 8
SEG = COLS // SEGMENTS
SEG_WIDE = SEG + 2 * STEPS
GROUPS = WIDE // 4
FIRST = 8
EXT = COLS + 2 * FIRST


def params(mib):
    return pltpu.CompilerParams(vmem_limit_bytes=mib * 1024 * 1024)


def took(us):
    return pl.CostEstimate(flops=int(us * 1.15e9), bytes_accessed=int(us * 1e6), transcendentals=0)


def in_hbm(a):
    return pltpu.with_memory_space_constraint(a, pltpu.HBM)


def nn(a, b):
    return lax.dot_general(a, b, (((1,), (0,)), ((), ())), preferred_element_type=F32)


def nt(a, b):
    return lax.dot_general(a, b, (((1,), (1,)), ((), ())), preferred_element_type=F32)


def iota(shape, dim):
    return lax.broadcasted_iota(jnp.int32, shape, dim)


def flipped(a):
    return a.astype(F32).T


def two_parts(a):
    high = a.astype(BF16)
    return high, (a - high.astype(F32)).astype(BF16)


def ranks(target):
    count = target.shape[1]
    tri = (iota((128, 128), 0) <= iota((128, 128), 1)).astype(F32).astype(BF16)
    carry = jnp.zeros((128, 1), F32)
    found = []
    for at in range(0, count, 128):
        hit = (iota((128, 128), 0) == target[:, at : at + 128]).astype(F32)
        upto = nn(hit.astype(BF16), tri) + carry
        carry = upto[:, 127:128]
        found.append(jnp.sum(hit * upto, axis=0, keepdims=True))
    return (jnp.concatenate(found, axis=1) - 1.0).astype(jnp.int32)


def keyed(target, rank):
    line = rank // ACROSS
    return LINES * target + line, rank - ACROSS * line


def key_hits(key, tiles):
    return (iota((LINES * tiles, key.shape[1]), 0) == key).astype(F32).astype(BF16)


def begin_kernel(comps, spec, total):
    found = nn(comps[...], spec[...])

    @pl.when(pl.program_id(0) == 0)
    def _():
        total[...] = found

    @pl.when(pl.program_id(0) > 0)
    def _():
        total[...] += found


def begin(comps, spec_t, steps):
    pcs, count = comps.shape[0], spec_t.shape[1]
    return pl.pallas_call(
        begin_kernel,
        grid=(steps,),
        in_specs=[
            pl.BlockSpec((pcs, BLOCK), lambda i: (0, i)),
            pl.BlockSpec((BLOCK, count), lambda i: (i, 0)),
        ],
        out_specs=pl.BlockSpec((pcs, count), lambda i: (0, 0)),
        out_shape=jax.ShapeDtypeStruct((pcs, count), F32),
        compiler_params=params(20), cost_estimate=took(4.5),
        name="begin",
    )(in_hbm(comps), in_hbm(spec_t))


def project_kernel(channels, done, target, cell, comps, spec, total, jac_t, weight, scores, send, sums):
    step = pl.program_id(0)
    steps = pl.num_programs(0)
    count = target.shape[1]
    tiles = send.shape[0]
    rest = channels - (pl.cdiv(channels, BLOCK) - 1) * BLOCK

    @pl.when(step == 0)
    def _():
        sums[...] = total[...] + nn(comps[...], spec[...])

    @pl.when(jnp.logical_and(step > 0, step < steps - 1))
    def _():
        sums[...] += nn(comps[...], spec[...])

    @pl.when(step == steps - 1)
    def _():
        found = (sums[...] + nn(comps[:, :rest], spec[:rest, :])).astype(BF16)
        scores[...] = found
        high, low = two_parts(flipped(jac_t[...]) * weight[...].reshape(1, -1))
        values = nn(high, found) + nn(low, found)
        rank = ranks(target[...])
        key, line = keyed(target[...], rank)
        values = jnp.concatenate([jnp.where(line == slot, values, 0.0) for slot in range(ACROSS)], axis=0)
        packed = nn(key_hits(key, tiles), values.T.astype(BF16))
        number = cell[...].reshape(1, count) + 1
        upper = number // SPLIT
        lower = number - upper * SPLIT
        lane = iota((128, count), 0)
        coded = jnp.where(lane == rank, upper, 0) + jnp.where(lane - SPLIT == rank, lower, 0)
        here = (iota((tiles, count), 0) == target[...]).astype(F32).astype(BF16)
        codes = nt(here, coded.astype(F32).astype(BF16)).astype(BF16)
        shape = (LINES * tiles, tiles)
        place = (iota(shape, 0) == LINES * iota(shape, 1) + CELL_LINE).astype(F32).astype(BF16)
        codes = nn(place, codes)
        for slot in range(ACROSS):
            cut = slice(slot * 128, slot * 128 + 128)
            full = packed[:, cut] + codes if slot == CELL_SLOT else packed[:, cut]
            send[:, :, cut] = full.astype(BF16).reshape(tiles, LINES, 128)


def project(target, cell, comps, spec_t, total, done, jac_t, weight, tiles):
    pcs, channels = comps.shape
    count = spec_t.shape[1]
    steps = pl.cdiv(channels, BLOCK) - done
    whole = lambda a: pl.BlockSpec(a.shape, lambda i: (0,) * a.ndim)
    return pl.pallas_call(
        functools.partial(project_kernel, channels, done),
        grid=(steps,),
        in_specs=[
            whole(target),
            whole(cell),
            pl.BlockSpec((pcs, BLOCK), lambda i: (0, i + done)),
            pl.BlockSpec((BLOCK, count), lambda i: (i + done, 0)),
            whole(total),
            whole(jac_t),
            whole(weight),
        ],
        out_specs=[
            pl.BlockSpec((pcs, count), lambda i: (0, 0)),
            pl.BlockSpec((tiles, LINES, ACROSS * 128), lambda i: (0, 0, 0)),
        ],
        out_shape=[
            pltpu.HBM((pcs, count), BF16),
            jax.ShapeDtypeStruct((tiles, LINES, ACROSS * 128), BF16),
        ],
        scratch_shapes=[pltpu.VMEM((pcs, count), F32)],
        compiler_params=params(20), cost_estimate=took(13),
        name="project",
    )(target, cell, in_hbm(comps), in_hbm(spec_t), total, jac_t, weight)


def strided(ref, first, count):
    return jnp.concatenate(
        [ref[pl.ds(first + at * ROWS, 8, stride=ROWS), :] for at in range(0, count, 8)], axis=0
    )


def lat_edges_kernel(inc, wind, turned, low, high):
    def turn(row, carry):
        turned[row] = strided(inc, row, FEATS).T
        return carry

    lax.fori_loop(0, ROWS, turn, 0)
    for at in range(STEPS):
        low[at, :FEATS] = turned[at]
        high[at, :FEATS] = turned[ROWS - STEPS + at]
        low[at, FEATS:] = strided(wind, at, 2 * LEVELS)
        high[at, FEATS:] = strided(wind, ROWS - STEPS + at, 2 * LEVELS)


def lat_edges(inc, wind):
    edge = jax.ShapeDtypeStruct((STEPS, FEATS + 2 * LEVELS, COLS), F32)
    return pl.pallas_call(
        lat_edges_kernel,
        out_shape=[jax.ShapeDtypeStruct((ROWS, COLS, FEATS), F32), edge, edge],
        compiler_params=params(6), cost_estimate=took(1.7),
        name="lat_edges",
    )(in_hbm(inc), in_hbm(wind))


def lon_edges_kernel(turned, wind, south, north, winds, low, high):
    for group in range(GROUPS):
        if group == 0:
            four = [south[at, FEATS:] for at in range(4)]
        elif group == GROUPS - 1:
            four = [north[at, FEATS:] for at in range(4)]
        else:
            four = [strided(wind, 4 * group - 4 + at, 2 * LEVELS) for at in range(4)]
        winds[group] = jnp.concatenate(four, axis=0).T
    for row in range(WIDE + GROUPS):
        place = slice(4 * row, 4 * row + 4)
        if row >= WIDE:
            low[place], high[place] = winds[row - WIDE, :4], winds[row - WIDE, COLS - 4 :]
        elif row < STEPS:
            low[place], high[place] = south[row, :4], south[row, COLS - 4 : COLS]
        elif row >= WIDE - STEPS:
            at = row - WIDE + STEPS
            low[place], high[place] = north[at, :4], north[at, COLS - 4 : COLS]
        else:
            low[place], high[place] = turned[row - STEPS, :4], turned[row - STEPS, COLS - 4 :]


def lon_edges(turned, wind, south, north):
    edge = jax.ShapeDtypeStruct((4 * (WIDE + GROUPS), 128), F32)
    return pl.pallas_call(
        lon_edges_kernel,
        out_shape=[jax.ShapeDtypeStruct((GROUPS, COLS, 128), F32), edge, edge],
        compiler_params=params(4), cost_estimate=took(0.3),
        name="lon_edges",
    )(turned, wind, south, north)


def spread(ext, row, full, west, east, mask):
    ext[row, FIRST - 4 : FIRST] = west * mask
    ext[row, FIRST : FIRST + COLS] = full * mask
    ext[row, FIRST + COLS : FIRST + COLS + 4] = east * mask


def segment(ext, row, col):
    return ext[row, pl.ds(FIRST - STEPS + col, SEGMENTS, stride=SEG), :]


def put_coefs(coefs, row, along, across, col, inside):
    coefs[row, col, 0] = (1.0 - along * along - across * across) * inside
    coefs[row, col, 1] = 0.5 * along * (1.0 + along)
    coefs[row, col, 2] = -0.5 * along * (1.0 - along)
    coefs[row, col, 3] = 0.5 * across * (1.0 + across)
    coefs[row, col, 4] = -0.5 * across * (1.0 - across)


def tangent_row(read, coefs, row, step, done):
    west, here = read(row, step - 1), read(row, step)
    for col in range(step, SEG_WIDE - step):
        east = read(row, col + 1)
        value = coefs[row, col, 0] * here + coefs[row, col, 1] * west + coefs[row, col, 2] * east
        value = value + coefs[row, col, 3] * read(row - 1, col) + coefs[row, col, 4] * read(row + 1, col)
        done(row, col, value)
        west, here = here, east


def adjoint_rows(read, coefs, row, step, done):
    def parts(at, col):
        value = read(row + at, col)
        return (value,) + tuple(coefs[row + at, col, i] * value for i in range(3))

    west = [parts(at, step - 1) for at in range(2)]
    here = [parts(at, step) for at in range(2)]
    for col in range(step, SEG_WIDE - step):
        east = [parts(at, col + 1) for at in range(2)]
        below = (read(row - 1, col), here[0][0])
        above = (here[1][0], read(row + 2, col))
        for at in range(2):
            value = here[at][1] + east[at][2] + west[at][3]
            value = value + coefs[row + at + 1, col, 3] * above[at] + coefs[row + at - 1, col, 4] * below[at]
            done(row + at, col, value)
        west, here = here, east


def sweep(some_rows, taken, ext, coefs, now, later, finish, after):
    source = lambda row, col: segment(ext, row, col)
    buffers = (now, later)
    for step in range(1, STEPS + 1):
        sink = buffers[step % 2]

        def advance(turn, carry, source=source, sink=sink, step=step):
            def keep(row, col, value):
                sink[row, col] = value

            some_rows(source, coefs, step + taken * turn, step, finish if step == STEPS else keep)
            if step == STEPS:
                after(turn)
            return carry

        lax.fori_loop(0, (WIDE - 2 * step) // taken, advance, 0)
        source = lambda row, col, sink=sink: sink[row, col]


def weigh_kernel(winds, west, east, coefs, ext, spot):
    band = lax.axis_index("lat")
    inside = [(band > 0).astype(F32), (band < lax.axis_size("lat") - 1).astype(F32)]
    lane = iota((128, 256), 1)
    for group in range(GROUPS):
        edge = slice(4 * (WIDE + group), 4 * (WIDE + group) + 4)
        spread(spot, 0, winds[group], west[edge], east[edge], 1.0)
        high, low = two_parts(spot[0])
        mask = inside[0] if group == 0 else inside[1] if group == GROUPS - 1 else 1.0
        for at in range(4):
            row = 4 * group + at
            source = 32 * at + LEVELS * (lane // 128) + lane % LEVELS
            copy = (iota((128, 256), 0) == source).astype(F32).astype(BF16)
            both = (nn(high, copy) + nn(low, copy)) * mask
            ext[0, row], ext[1, row] = both[:, :128], both[:, 128:]

    def weigh(row, carry):
        mask = jnp.where(row < STEPS, inside[0], jnp.where(row >= WIDE - STEPS, inside[1], 1.0))
        for col in range(SEG_WIDE):
            along, across = segment(ext.at[0], row, col), segment(ext.at[1], row, col)
            put_coefs(coefs, row, along, across, col, mask)
        return carry

    lax.fori_loop(0, WIDE, weigh, 0)


def weigh(winds, west, east):
    return pl.pallas_call(
        weigh_kernel,
        out_shape=jax.ShapeDtypeStruct((WIDE, SEG_WIDE, 5, 8, 128), F32),
        scratch_shapes=[pltpu.VMEM((2, WIDE, EXT, 128), F32), pltpu.VMEM((1, EXT, 128), F32)],
        compiler_params=params(6), cost_estimate=took(3.3),
        name="weigh",
    )(winds, west, east)


def tangent_kernel(turned, south, north, west, east, coefs, jac_t, weight, state, changed, ext, now, later):
    band = lax.axis_index("lat")
    inside = [(band > 0).astype(F32), (band < lax.axis_size("lat") - 1).astype(F32)]
    for row in range(WIDE):
        edge = slice(4 * row, 4 * row + 4)
        if row < STEPS:
            spread(ext, row, south[row, :FEATS], west[edge], east[edge], inside[0])
        elif row >= WIDE - STEPS:
            spread(ext, row, north[row - WIDE + STEPS, :FEATS], west[edge], east[edge], inside[1])
        else:
            spread(ext, row, turned[row - STEPS], west[edge], east[edge], 1.0)

    def finish(row, col, value):
        changed[row - STEPS, pl.ds(col - STEPS, SEGMENTS, stride=SEG), :] = value

    sweep(tangent_row, 1, ext, coefs, now, later, finish, lambda turn: None)
    high, low = two_parts(flipped(jac_t[...]) * weight[...].reshape(1, -1))
    high, low = two_parts(nn(high, jac_t[...]) + nn(low, jac_t[...]))
    for row in range(ROWS):
        full = changed[row].astype(BF16)
        state[row] = full
    state[ROWS], state[ROWS + 1] = high, low


def tangent(turned, south, north, west, east, coefs, jac_t, weight):
    return pl.pallas_call(
        tangent_kernel,
        out_shape=jax.ShapeDtypeStruct((ROWS + 2, COLS, FEATS), BF16),
        scratch_shapes=[
            pltpu.VMEM((ROWS, COLS, FEATS), F32),
            pltpu.VMEM((WIDE, EXT, 128), F32),
            pltpu.VMEM((WIDE, SEG_WIDE, 8, 128), F32),
            pltpu.VMEM((WIDE, SEG_WIDE, 8, 128), F32),
        ],
        compiler_params=params(10), cost_estimate=took(4.8),
        name="tangent",
    )(turned, south, north, west, east, coefs, jac_t, weight)


def slot_of(message, slot):
    cut = message[:, :, slot * 128 : slot * 128 + 128]
    return cut.reshape(cut.shape[0] * LINES, 128)


def slot_codes(got, slot):
    rows = got.shape[0] * LINES
    coded = slot_of(got, CELL_SLOT).astype(F32).reshape(got.shape[0], LINES, 128)[:, CELL_LINE : CELL_LINE + 1]
    coded = jnp.broadcast_to(coded, (got.shape[0], LINES, 128)).reshape(rows, 128)
    lane = iota((rows, 128), 1) % SPLIT
    return jnp.where(lane == iota((rows, 128), 0) % LINES * ACROSS + slot, coded, 0.0).astype(BF16)


def code_weights(shape, dim):
    return jnp.where(iota(shape, dim) < SPLIT, float(SPLIT), 1.0).astype(BF16)


def place_of(cells):
    upper = jnp.floor(cells * (1.0 / COLS))
    return upper, cells - upper * COLS


def gather_kernel(got, state, send):
    rows = got.shape[0] * LINES
    field = state[:ROWS].reshape(ROWS * COLS, FEATS)
    lane = iota((rows, 128), 1).astype(F32)
    none = jnp.zeros((rows, 128), BF16)
    for slot in range(ACROSS):
        cells = nn(slot_codes(got, slot), code_weights((128, 128), 0)) - 1.0
        upper, column = place_of(cells)
        upper = upper.astype(BF16)
        along = (column == lane).astype(F32).astype(BF16)
        hits = jnp.concatenate([jnp.where(upper == jnp.bfloat16(row), along, none) for row in range(ROWS)], axis=1)
        found = nn(hits, field).astype(BF16)
        send[:, :, slot * 128 : slot * 128 + 128] = found.reshape(got.shape[0], LINES, 128)


def gather(got, state):
    return pl.pallas_call(
        gather_kernel,
        out_shape=jax.ShapeDtypeStruct(got.shape, BF16),
        compiler_params=params(10), cost_estimate=took(3.9),
        name="gather",
    )(got, state)


def scatter_kernel(got, state, forcing, low, high):
    rows = got.shape[0] * LINES
    cells = jnp.concatenate(
        [nt(code_weights((16, 128), 1), slot_codes(got, slot))[:1] - 1.0 for slot in range(ACROSS)], axis=1
    )
    terms = jnp.concatenate([slot_of(got, slot) for slot in range(ACROSS)], axis=0)
    terms = jnp.concatenate([terms, jnp.ones(terms.shape, BF16)], axis=1)
    shape = (COLS, ACROSS * rows)
    upper, column = place_of(cells)
    along = (iota(shape, 0).astype(F32) == column).astype(F32).astype(BF16)
    upper = jnp.broadcast_to(upper, shape).astype(BF16)
    none = jnp.zeros(shape, BF16)
    change = jnp.concatenate([state[ROWS], state[ROWS + 1]], axis=1)
    for first in range(0, ROWS, MANY):
        hits = [jnp.where(upper == jnp.bfloat16(first + at), along, none) for at in range(MANY)]
        found = nn(jnp.concatenate(hits, axis=0), terms)
        changed = nn(state[first : first + MANY].reshape(MANY * COLS, FEATS), change)
        changed = changed[:, :FEATS] + changed[:, FEATS:]
        full = (found[:, :FEATS] - found[:, FEATS:] * changed).reshape(MANY, COLS, FEATS)
        forcing[first : first + MANY] = full
        if first == 0:
            low[...] = full[:STEPS].astype(BF16)
        if first + MANY == ROWS:
            high[...] = full[MANY - STEPS :].astype(BF16)


def scatter(got, state):
    edge = jax.ShapeDtypeStruct((STEPS, COLS, FEATS), BF16)
    return pl.pallas_call(
        scatter_kernel,
        out_shape=[jax.ShapeDtypeStruct((ROWS, COLS, FEATS), F32), edge, edge],
        compiler_params=params(14), cost_estimate=took(3.7),
        name="scatter",
    )(got, state)


def forcing_edges_kernel(forcing, south, north, low, high):
    first, last = [], []
    for row in range(WIDE):
        if row < STEPS:
            full = south[row].astype(F32)
        elif row >= WIDE - STEPS:
            full = north[row - WIDE + STEPS].astype(F32)
        else:
            full = forcing[row - STEPS]
        first.append(full[:4])
        last.append(full[COLS - 4 :])
    low[...] = jnp.concatenate(first, axis=0).astype(BF16)
    high[...] = jnp.concatenate(last, axis=0).astype(BF16)


def forcing_edges(forcing, south, north):
    edge = jax.ShapeDtypeStruct((4 * WIDE, FEATS), BF16)
    return pl.pallas_call(
        forcing_edges_kernel, out_shape=[edge, edge], compiler_params=params(4), cost_estimate=took(0.3), name="forcing_edges"
    )(forcing, south, north)


def adjoint_kernel(inc, coefs, forcing, south, north, west, east, out, ext, back, now, later):
    left, right = west[...].astype(F32), east[...].astype(F32)
    for row in range(WIDE):
        if row < STEPS:
            full = south[row].astype(F32)
        elif row >= WIDE - STEPS:
            full = north[row - WIDE + STEPS].astype(F32)
        else:
            full = forcing[row - STEPS]
        edge = slice(4 * row, 4 * row + 4)
        spread(ext, row, full, left[edge], right[edge], 1.0)

    def finish(row, col, value):
        back[row - STEPS, pl.ds(col - STEPS, SEGMENTS, stride=SEG), :] = value

    def turn(row):
        full = back[row].T
        for at in range(0, FEATS, 8):
            place = pl.ds(at * ROWS + row, 8, stride=ROWS)
            out[place, :] = inc[place, :] - full[at : at + 8]

    def behind(pair):
        first = 2 * jnp.maximum(pair - 1, 0)
        turn(first)
        turn(first + 1)

    sweep(adjoint_rows, 2, ext, coefs, now, later, finish, behind)
    turn(ROWS - 2)
    turn(ROWS - 1)


def adjoint(inc, coefs, forcing, south, north, west, east):
    return pl.pallas_call(
        adjoint_kernel,
        out_shape=jax.ShapeDtypeStruct(inc.shape, F32),
        scratch_shapes=[
            pltpu.VMEM((WIDE, EXT, 128), F32),
            pltpu.VMEM((ROWS, COLS, FEATS), F32),
            pltpu.VMEM((WIDE, SEG_WIDE, 8, 128), F32),
            pltpu.VMEM((WIDE, SEG_WIDE, 8, 128), F32),
        ],
        compiler_params=params(10), cost_estimate=took(7),
        name="adjoint",
    )(inc, coefs, forcing, south, north, west, east)


def depart_kernel(target, back, scores, jac_t, weight, out):
    tiles = back.shape[0]
    pcs, count = scores.shape
    key, rest = keyed(target[...], ranks(target[...]))
    sent = jnp.concatenate([flipped(slot_of(back, slot)).astype(BF16) for slot in range(ACROSS)], axis=0)
    found = nn(sent, key_hits(key, tiles))
    column = jnp.zeros((FEATS, count), F32)
    for slot in range(ACROSS):
        column = jnp.where(rest == slot, found[slot * FEATS : (slot + 1) * FEATS], column)
    scale = jnp.broadcast_to(weight[...].reshape(1, -1), (128, pcs)).T
    column = column.astype(BF16)
    for at in range(0, count, 128):
        model = nn(jac_t[...], column[:, at : at + 128])
        cut = slice(at, at + 128)
        out[:, cut] = (scale * (scores[:, cut].astype(F32) - model)).astype(BF16)


def depart(target, back, scores, jac_t, weight):
    return pl.pallas_call(
        depart_kernel,
        out_shape=jax.ShapeDtypeStruct(scores.shape, BF16),
        compiler_params=params(10), cost_estimate=took(3.5),
        name="depart",
    )(target, back, scores, jac_t, weight)


def ring(value, axis, move):
    count = lax.axis_size(axis)
    return lax.ppermute(value, axis, [(i, (i + move) % count) for i in range(count)])


def swapped(value):
    return lax.all_to_all(value, ("lat", "lon"), split_axis=0, concat_axis=0, tiled=True)


def shards(increment, courant, spectra, components, jacobian, obs_weight, tile_target, tile_cell):
    tiles = lax.axis_size("lat") * lax.axis_size("lon")
    count = spectra.shape[0]
    inc = increment.reshape(FEATS * ROWS, COLS)
    wind = courant.reshape(2 * LEVELS * ROWS, COLS)
    target = tile_target.reshape(1, count)
    cell = tile_cell
    jac_t = jacobian.T
    weight = obs_weight

    turned, low, high = lat_edges(inc, wind)
    south = ring(high, "lat", 1)
    north = ring(low, "lat", -1)
    total = begin(components, spectra.T, EARLY)
    total, south, north = lax.optimization_barrier((total, south, north))
    winds, low, high = lon_edges(turned, wind, south, north)
    west = ring(high, "lon", 1)
    east = ring(low, "lon", -1)
    scores, send = project(target, cell, components, spectra.T, total, EARLY, jac_t, weight, tiles)
    send, west, east = lax.optimization_barrier((send, west, east))
    got = swapped(send)
    coefs = weigh(winds, west, east)
    state = tangent(turned, south, north, west, east, coefs, jac_t, weight)

    send = gather(got, state)
    forcing, low, high = scatter(got, state)
    south = ring(high, "lat", 1)
    north = ring(low, "lat", -1)
    send, forcing = lax.optimization_barrier((send, forcing))
    back = swapped(send)
    low, winds = lax.optimization_barrier((low, winds))
    coefs = weigh(winds, west, east)
    low, high = forcing_edges(forcing, south, north)
    west = ring(high, "lon", 1)
    east = ring(low, "lon", -1)
    gradient = adjoint(inc, coefs, forcing, south, north, west, east)

    departures = depart(target, back, scores, jac_t, weight)
    return gradient.reshape(increment.shape), departures.T


def solution(mesh):
    placed = (
        P(None, None, "lat", "lon"),
        P(None, None, "lat", "lon"),
        P(("lat", "lon"), None),
        P(),
        P(),
        P(),
        P(("lat", "lon"), None),
        P(("lat", "lon")),
    )
    return jax.shard_map(
        shards,
        mesh=mesh,
        in_specs=placed,
        out_specs=(P(None, None, "lat", "lon"), P(("lat", "lon"), None)),
        check_vma=False,
    )
```

```python
import functools

import jax
import jax.numpy as jnp
from jax import lax
from jax.experimental import pallas as pl
from jax.experimental.pallas import tpu as pltpu
from jax.sharding import PartitionSpec as P

F32 = jnp.float32
BF16 = jnp.bfloat16
TRACERS, LEVELS, ROWS, COLS = 8, 16, 16, 128
FEATS = TRACERS * LEVELS
STEPS = 4
WIDE = ROWS + 2 * STEPS
CAP = 18
LINES, ACROSS = 4, 5
CELL_LINE, CELL_SLOT = CAP // ACROSS, CAP % ACROSS
BACK = (2, CAP // 2)
SPLIT = 64
BLOCK = 1280
EARLY = 2
MANY = 4
SEGMENTS = 8
SEG = COLS // SEGMENTS
SEG_WIDE = SEG + 2 * STEPS
GROUPS = WIDE // 4
FIRST = 8
EXT = COLS + 2 * FIRST


def params(mib):
    return pltpu.CompilerParams(vmem_limit_bytes=mib * 1024 * 1024)


def took(us):
    return pl.CostEstimate(flops=int(us * 1.15e9), bytes_accessed=int(us * 1e6), transcendentals=0)


def in_hbm(a):
    return pltpu.with_memory_space_constraint(a, pltpu.HBM)


def nn(a, b):
    return lax.dot_general(a, b, (((1,), (0,)), ((), ())), preferred_element_type=F32)


def nt(a, b):
    return lax.dot_general(a, b, (((1,), (1,)), ((), ())), preferred_element_type=F32)


def iota(shape, dim):
    return lax.broadcasted_iota(jnp.int32, shape, dim)


def flipped(a):
    return a.astype(F32).T


def two_parts(a):
    high = a.astype(BF16)
    return high, (a - high.astype(F32)).astype(BF16)


def ranks(target):
    count = target.shape[1]
    tri = (iota((128, 128), 0) <= iota((128, 128), 1)).astype(F32).astype(BF16)
    carry = jnp.zeros((128, 1), F32)
    found = []
    for at in range(0, count, 128):
        hit = (iota((128, 128), 0) == target[:, at : at + 128]).astype(F32)
        upto = nn(hit.astype(BF16), tri) + carry
        carry = upto[:, 127:128]
        found.append(jnp.sum(hit * upto, axis=0, keepdims=True))
    return (jnp.concatenate(found, axis=1) - 1.0).astype(jnp.int32)


def keyed(target, rank, lines=LINES, across=ACROSS):
    line = rank // across
    return lines * target + line, rank - across * line


def key_hits(key, rows):
    return (iota((rows, key.shape[1]), 0) == key).astype(F32).astype(BF16)


def begin_kernel(comps, spec, total):
    found = nn(comps[...], spec[...])

    @pl.when(pl.program_id(0) == 0)
    def _():
        total[...] = found

    @pl.when(pl.program_id(0) > 0)
    def _():
        total[...] += found


def begin(comps, spec_t, steps):
    pcs, count = comps.shape[0], spec_t.shape[1]
    return pl.pallas_call(
        begin_kernel,
        grid=(steps,),
        in_specs=[
            pl.BlockSpec((pcs, BLOCK), lambda i: (0, i)),
            pl.BlockSpec((BLOCK, count), lambda i: (i, 0)),
        ],
        out_specs=pl.BlockSpec((pcs, count), lambda i: (0, 0)),
        out_shape=jax.ShapeDtypeStruct((pcs, count), F32),
        compiler_params=params(20), cost_estimate=took(4.5),
        name="begin",
    )(in_hbm(comps), in_hbm(spec_t))


def project_kernel(channels, done, target, cell, comps, spec, total, jac_t, weight, scores, send, sums):
    step = pl.program_id(0)
    steps = pl.num_programs(0)
    count = target.shape[1]
    tiles = send.shape[0]
    rest = channels - (pl.cdiv(channels, BLOCK) - 1) * BLOCK

    @pl.when(step == 0)
    def _():
        sums[...] = total[...] + nn(comps[...], spec[...])

    @pl.when(jnp.logical_and(step > 0, step < steps - 1))
    def _():
        sums[...] += nn(comps[...], spec[...])

    @pl.when(step == steps - 1)
    def _():
        found = (sums[...] + nn(comps[:, :rest], spec[:rest, :])).astype(BF16)
        scores[...] = found
        high, low = two_parts(flipped(jac_t[...]) * weight[...].reshape(1, -1))
        values = nn(high, found) + nn(low, found)
        rank = ranks(target[...])
        key, line = keyed(target[...], rank)
        values = jnp.concatenate([jnp.where(line == slot, values, 0.0) for slot in range(ACROSS)], axis=0)
        packed = nn(key_hits(key, LINES * tiles), values.T.astype(BF16))
        number = cell[...].reshape(1, count) + 1
        upper = number // SPLIT
        lower = number - upper * SPLIT
        lane = iota((128, count), 0)
        coded = jnp.where(lane == rank, upper, 0) + jnp.where(lane - SPLIT == rank, lower, 0)
        here = (iota((tiles, count), 0) == target[...]).astype(F32).astype(BF16)
        codes = nt(here, coded.astype(F32).astype(BF16)).astype(BF16)
        shape = (LINES * tiles, tiles)
        place = (iota(shape, 0) == LINES * iota(shape, 1) + CELL_LINE).astype(F32).astype(BF16)
        codes = nn(place, codes)
        for slot in range(ACROSS):
            cut = slice(slot * 128, slot * 128 + 128)
            full = packed[:, cut] + codes if slot == CELL_SLOT else packed[:, cut]
            send[:, :, cut] = full.astype(BF16).reshape(tiles, LINES, 128)


def project(target, cell, comps, spec_t, total, done, jac_t, weight, tiles):
    pcs, channels = comps.shape
    count = spec_t.shape[1]
    steps = pl.cdiv(channels, BLOCK) - done
    whole = lambda a: pl.BlockSpec(a.shape, lambda i: (0,) * a.ndim)
    return pl.pallas_call(
        functools.partial(project_kernel, channels, done),
        grid=(steps,),
        in_specs=[
            whole(target),
            whole(cell),
            pl.BlockSpec((pcs, BLOCK), lambda i: (0, i + done)),
            pl.BlockSpec((BLOCK, count), lambda i: (i + done, 0)),
            whole(total),
            whole(jac_t),
            whole(weight),
        ],
        out_specs=[
            pl.BlockSpec((pcs, count), lambda i: (0, 0)),
            pl.BlockSpec((tiles, LINES, ACROSS * 128), lambda i: (0, 0, 0)),
        ],
        out_shape=[
            pltpu.HBM((pcs, count), BF16),
            jax.ShapeDtypeStruct((tiles, LINES, ACROSS * 128), BF16),
        ],
        scratch_shapes=[pltpu.VMEM((pcs, count), F32)],
        compiler_params=params(20), cost_estimate=took(13),
        name="project",
    )(target, cell, in_hbm(comps), in_hbm(spec_t), total, jac_t, weight)


def strided(ref, first, count):
    return jnp.concatenate(
        [ref[pl.ds(first + at * ROWS, 8, stride=ROWS), :] for at in range(0, count, 8)], axis=0
    )


def lat_edges_kernel(inc, wind, turned, low, high):
    def turn(row, carry):
        turned[row] = strided(inc, row, FEATS).T
        return carry

    lax.fori_loop(0, ROWS, turn, 0)
    for at in range(STEPS):
        low[at, :FEATS] = turned[at]
        high[at, :FEATS] = turned[ROWS - STEPS + at]
        low[at, FEATS:] = strided(wind, at, 2 * LEVELS)
        high[at, FEATS:] = strided(wind, ROWS - STEPS + at, 2 * LEVELS)


def lat_edges(inc, wind):
    edge = jax.ShapeDtypeStruct((STEPS, FEATS + 2 * LEVELS, COLS), F32)
    return pl.pallas_call(
        lat_edges_kernel,
        out_shape=[jax.ShapeDtypeStruct((ROWS, COLS, FEATS), F32), edge, edge],
        compiler_params=params(6), cost_estimate=took(1.7),
        name="lat_edges",
    )(in_hbm(inc), in_hbm(wind))


def lon_edges_kernel(turned, wind, south, north, winds, low, high):
    for group in range(GROUPS):
        if group == 0:
            four = [south[at, FEATS:] for at in range(4)]
        elif group == GROUPS - 1:
            four = [north[at, FEATS:] for at in range(4)]
        else:
            four = [strided(wind, 4 * group - 4 + at, 2 * LEVELS) for at in range(4)]
        winds[group] = jnp.concatenate(four, axis=0).T
    for row in range(WIDE + GROUPS):
        place = slice(4 * row, 4 * row + 4)
        if row >= WIDE:
            low[place], high[place] = winds[row - WIDE, :4], winds[row - WIDE, COLS - 4 :]
        elif row < STEPS:
            low[place], high[place] = south[row, :4], south[row, COLS - 4 : COLS]
        elif row >= WIDE - STEPS:
            at = row - WIDE + STEPS
            low[place], high[place] = north[at, :4], north[at, COLS - 4 : COLS]
        else:
            low[place], high[place] = turned[row - STEPS, :4], turned[row - STEPS, COLS - 4 :]


def lon_edges(turned, wind, south, north):
    edge = jax.ShapeDtypeStruct((4 * (WIDE + GROUPS), 128), F32)
    return pl.pallas_call(
        lon_edges_kernel,
        out_shape=[jax.ShapeDtypeStruct((GROUPS, COLS, 128), F32), edge, edge],
        compiler_params=params(4), cost_estimate=took(0.3),
        name="lon_edges",
    )(turned, wind, south, north)


def spread(ext, row, full, west, east, mask):
    ext[row, FIRST - 4 : FIRST] = west * mask
    ext[row, FIRST : FIRST + COLS] = full * mask
    ext[row, FIRST + COLS : FIRST + COLS + 4] = east * mask


def segment(ext, row, col):
    return ext[row, pl.ds(FIRST - STEPS + col, SEGMENTS, stride=SEG), :]


def put_coefs(coefs, row, along, across, col, inside):
    coefs[row, col, 0] = (1.0 - along * along - across * across) * inside
    coefs[row, col, 1] = 0.5 * along * (1.0 + along)
    coefs[row, col, 2] = -0.5 * along * (1.0 - along)
    coefs[row, col, 3] = 0.5 * across * (1.0 + across)
    coefs[row, col, 4] = -0.5 * across * (1.0 - across)


def tangent_row(read, coefs, row, step, done):
    west, here = read(row, step - 1), read(row, step)
    for col in range(step, SEG_WIDE - step):
        east = read(row, col + 1)
        value = coefs[row, col, 0] * here + coefs[row, col, 1] * west + coefs[row, col, 2] * east
        value = value + coefs[row, col, 3] * read(row - 1, col) + coefs[row, col, 4] * read(row + 1, col)
        done(row, col, value)
        west, here = here, east


def adjoint_rows(read, coefs, row, step, done):
    def parts(at, col):
        value = read(row + at, col)
        return (value,) + tuple(coefs[row + at, col, i] * value for i in range(3))

    west = [parts(at, step - 1) for at in range(2)]
    here = [parts(at, step) for at in range(2)]
    for col in range(step, SEG_WIDE - step):
        east = [parts(at, col + 1) for at in range(2)]
        below = (read(row - 1, col), here[0][0])
        above = (here[1][0], read(row + 2, col))
        for at in range(2):
            value = here[at][1] + east[at][2] + west[at][3]
            value = value + coefs[row + at + 1, col, 3] * above[at] + coefs[row + at - 1, col, 4] * below[at]
            done(row + at, col, value)
        west, here = here, east


def sweep(some_rows, taken, ext, coefs, now, later, finish, after):
    source = lambda row, col: segment(ext, row, col)
    buffers = (now, later)
    for step in range(1, STEPS + 1):
        sink = buffers[step % 2]

        def advance(turn, carry, source=source, sink=sink, step=step):
            def keep(row, col, value):
                sink[row, col] = value

            some_rows(source, coefs, step + taken * turn, step, finish if step == STEPS else keep)
            if step == STEPS:
                after(turn)
            return carry

        lax.fori_loop(0, (WIDE - 2 * step) // taken, advance, 0)
        source = lambda row, col, sink=sink: sink[row, col]


def weigh_kernel(winds, west, east, coefs, ext, spot):
    band = lax.axis_index("lat")
    inside = [(band > 0).astype(F32), (band < lax.axis_size("lat") - 1).astype(F32)]
    lane = iota((128, 256), 1)
    for group in range(GROUPS):
        edge = slice(4 * (WIDE + group), 4 * (WIDE + group) + 4)
        spread(spot, 0, winds[group], west[edge], east[edge], 1.0)
        high, low = two_parts(spot[0])
        mask = inside[0] if group == 0 else inside[1] if group == GROUPS - 1 else 1.0
        for at in range(4):
            row = 4 * group + at
            source = 32 * at + LEVELS * (lane // 128) + lane % LEVELS
            copy = (iota((128, 256), 0) == source).astype(F32).astype(BF16)
            both = (nn(high, copy) + nn(low, copy)) * mask
            ext[0, row], ext[1, row] = both[:, :128], both[:, 128:]

    def weigh(row, carry):
        mask = jnp.where(row < STEPS, inside[0], jnp.where(row >= WIDE - STEPS, inside[1], 1.0))
        for col in range(SEG_WIDE):
            along, across = segment(ext.at[0], row, col), segment(ext.at[1], row, col)
            put_coefs(coefs, row, along, across, col, mask)
        return carry

    lax.fori_loop(0, WIDE, weigh, 0)


def weigh(winds, west, east):
    return pl.pallas_call(
        weigh_kernel,
        out_shape=jax.ShapeDtypeStruct((WIDE, SEG_WIDE, 5, 8, 128), F32),
        scratch_shapes=[pltpu.VMEM((2, WIDE, EXT, 128), F32), pltpu.VMEM((1, EXT, 128), F32)],
        compiler_params=params(6), cost_estimate=took(3.3),
        name="weigh",
    )(winds, west, east)


def tangent_kernel(turned, south, north, west, east, coefs, jac_t, weight, state, changed, ext, now, later):
    band = lax.axis_index("lat")
    inside = [(band > 0).astype(F32), (band < lax.axis_size("lat") - 1).astype(F32)]
    for row in range(WIDE):
        edge = slice(4 * row, 4 * row + 4)
        if row < STEPS:
            spread(ext, row, south[row, :FEATS], west[edge], east[edge], inside[0])
        elif row >= WIDE - STEPS:
            spread(ext, row, north[row - WIDE + STEPS, :FEATS], west[edge], east[edge], inside[1])
        else:
            spread(ext, row, turned[row - STEPS], west[edge], east[edge], 1.0)

    def finish(row, col, value):
        changed[row - STEPS, pl.ds(col - STEPS, SEGMENTS, stride=SEG), :] = value

    sweep(tangent_row, 1, ext, coefs, now, later, finish, lambda turn: None)
    high, low = two_parts(flipped(jac_t[...]) * weight[...].reshape(1, -1))
    high, low = two_parts(nn(high, jac_t[...]) + nn(low, jac_t[...]))
    for row in range(ROWS):
        full = changed[row].astype(BF16)
        state[row] = full
    state[ROWS], state[ROWS + 1] = high, low


def tangent(turned, south, north, west, east, coefs, jac_t, weight):
    return pl.pallas_call(
        tangent_kernel,
        out_shape=jax.ShapeDtypeStruct((ROWS + 2, COLS, FEATS), BF16),
        scratch_shapes=[
            pltpu.VMEM((ROWS, COLS, FEATS), F32),
            pltpu.VMEM((WIDE, EXT, 128), F32),
            pltpu.VMEM((WIDE, SEG_WIDE, 8, 128), F32),
            pltpu.VMEM((WIDE, SEG_WIDE, 8, 128), F32),
        ],
        compiler_params=params(10), cost_estimate=took(4.8),
        name="tangent",
    )(turned, south, north, west, east, coefs, jac_t, weight)


def slot_of(message, slot):
    cut = message[:, :, slot * 128 : slot * 128 + 128]
    return cut.reshape(cut.shape[0] * cut.shape[1], 128)


def slot_codes(got, slot, lines=LINES, across=ACROSS):
    tiles = got.shape[0]
    rows = tiles * lines
    coded = slot_of(got, CELL_SLOT).astype(F32).reshape(tiles, LINES, 128)[:, CELL_LINE : CELL_LINE + 1]
    coded = jnp.broadcast_to(coded, (tiles, lines, 128)).reshape(rows, 128)
    lane = iota((rows, 128), 1) % SPLIT
    return jnp.where(lane == iota((rows, 128), 0) % lines * across + slot, coded, 0.0).astype(BF16)


def code_weights(shape, dim):
    return jnp.where(iota(shape, dim) < SPLIT, float(SPLIT), 1.0).astype(BF16)


def place_of(cells):
    upper = jnp.floor(cells * (1.0 / COLS))
    return upper, cells - upper * COLS


def gather_kernel(got, state, send):
    rows = got.shape[0] * BACK[0]
    field = state[:ROWS].reshape(ROWS * COLS, FEATS)
    lane = iota((rows, 128), 1).astype(F32)
    none = jnp.zeros((rows, 128), BF16)
    for slot in range(BACK[1]):
        cells = nn(slot_codes(got, slot, *BACK), code_weights((128, 128), 0)) - 1.0
        upper, column = place_of(cells)
        upper = upper.astype(BF16)
        along = (column == lane).astype(F32).astype(BF16)
        hits = jnp.concatenate([jnp.where(upper == jnp.bfloat16(row), along, none) for row in range(ROWS)], axis=1)
        found = nn(hits, field).astype(BF16)
        send[:, :, slot * 128 : slot * 128 + 128] = found.reshape(got.shape[0], BACK[0], 128)


def gather(got, state):
    return pl.pallas_call(
        gather_kernel,
        out_shape=jax.ShapeDtypeStruct((got.shape[0], BACK[0], BACK[1] * 128), BF16),
        compiler_params=params(10), cost_estimate=took(3.9),
        name="gather",
    )(got, state)


def scatter_kernel(got, state, forcing, low, high):
    rows = got.shape[0] * LINES
    cells = jnp.concatenate(
        [nt(code_weights((16, 128), 1), slot_codes(got, slot))[:1] - 1.0 for slot in range(ACROSS)], axis=1
    )
    terms = jnp.concatenate([slot_of(got, slot) for slot in range(ACROSS)], axis=0)
    terms = jnp.concatenate([terms, jnp.ones(terms.shape, BF16)], axis=1)
    shape = (COLS, ACROSS * rows)
    upper, column = place_of(cells)
    along = (iota(shape, 0).astype(F32) == column).astype(F32).astype(BF16)
    upper = jnp.broadcast_to(upper, shape).astype(BF16)
    none = jnp.zeros(shape, BF16)
    change = jnp.concatenate([state[ROWS], state[ROWS + 1]], axis=1)
    for first in range(0, ROWS, MANY):
        hits = [jnp.where(upper == jnp.bfloat16(first + at), along, none) for at in range(MANY)]
        found = nn(jnp.concatenate(hits, axis=0), terms)
        changed = nn(state[first : first + MANY].reshape(MANY * COLS, FEATS), change)
        changed = changed[:, :FEATS] + changed[:, FEATS:]
        full = (found[:, :FEATS] - found[:, FEATS:] * changed).reshape(MANY, COLS, FEATS)
        forcing[first : first + MANY] = full
        if first == 0:
            low[...] = full[:STEPS].astype(BF16)
        if first + MANY == ROWS:
            high[...] = full[MANY - STEPS :].astype(BF16)


def scatter(got, state):
    edge = jax.ShapeDtypeStruct((STEPS, COLS, FEATS), BF16)
    return pl.pallas_call(
        scatter_kernel,
        out_shape=[jax.ShapeDtypeStruct((ROWS, COLS, FEATS), F32), edge, edge],
        compiler_params=params(14), cost_estimate=took(3.7),
        name="scatter",
    )(got, state)


def forcing_edges_kernel(forcing, south, north, low, high):
    first, last = [], []
    for row in range(WIDE):
        if row < STEPS:
            full = south[row].astype(F32)
        elif row >= WIDE - STEPS:
            full = north[row - WIDE + STEPS].astype(F32)
        else:
            full = forcing[row - STEPS]
        first.append(full[:4])
        last.append(full[COLS - 4 :])
    low[...] = jnp.concatenate(first, axis=0).astype(BF16)
    high[...] = jnp.concatenate(last, axis=0).astype(BF16)


def forcing_edges(forcing, south, north):
    edge = jax.ShapeDtypeStruct((4 * WIDE, FEATS), BF16)
    return pl.pallas_call(
        forcing_edges_kernel, out_shape=[edge, edge], compiler_params=params(4), cost_estimate=took(0.3), name="forcing_edges"
    )(forcing, south, north)


def adjoint_kernel(inc, coefs, forcing, south, north, west, east, out, ext, back, now, later):
    left, right = west[...].astype(F32), east[...].astype(F32)
    for row in range(WIDE):
        if row < STEPS:
            full = south[row].astype(F32)
        elif row >= WIDE - STEPS:
            full = north[row - WIDE + STEPS].astype(F32)
        else:
            full = forcing[row - STEPS]
        edge = slice(4 * row, 4 * row + 4)
        spread(ext, row, full, left[edge], right[edge], 1.0)

    def finish(row, col, value):
        back[row - STEPS, pl.ds(col - STEPS, SEGMENTS, stride=SEG), :] = value

    def turn(row):
        full = back[row].T
        for at in range(0, FEATS, 8):
            place = pl.ds(at * ROWS + row, 8, stride=ROWS)
            out[place, :] = inc[place, :] - full[at : at + 8]

    def behind(pair):
        first = 2 * jnp.maximum(pair - 1, 0)
        turn(first)
        turn(first + 1)

    sweep(adjoint_rows, 2, ext, coefs, now, later, finish, behind)
    turn(ROWS - 2)
    turn(ROWS - 1)


def adjoint(inc, coefs, forcing, south, north, west, east):
    return pl.pallas_call(
        adjoint_kernel,
        out_shape=jax.ShapeDtypeStruct(inc.shape, F32),
        scratch_shapes=[
            pltpu.VMEM((WIDE, EXT, 128), F32),
            pltpu.VMEM((ROWS, COLS, FEATS), F32),
            pltpu.VMEM((WIDE, SEG_WIDE, 8, 128), F32),
            pltpu.VMEM((WIDE, SEG_WIDE, 8, 128), F32),
        ],
        compiler_params=params(10), cost_estimate=took(7),
        name="adjoint",
    )(inc, coefs, forcing, south, north, west, east)


def depart_kernel(target, back, scores, jac_t, weight, out):
    tiles = back.shape[0]
    pcs, count = scores.shape
    key, rest = keyed(target[...], ranks(target[...]), *BACK)
    sent = jnp.concatenate([flipped(slot_of(back, slot)).astype(BF16) for slot in range(BACK[1])], axis=0)
    found = nn(sent, key_hits(key, BACK[0] * tiles))
    column = jnp.zeros((FEATS, count), F32)
    for slot in range(BACK[1]):
        column = jnp.where(rest == slot, found[slot * FEATS : (slot + 1) * FEATS], column)
    scale = jnp.broadcast_to(weight[...].reshape(1, -1), (128, pcs)).T
    column = column.astype(BF16)
    for at in range(0, count, 128):
        model = nn(jac_t[...], column[:, at : at + 128])
        cut = slice(at, at + 128)
        out[:, cut] = (scale * (scores[:, cut].astype(F32) - model)).astype(BF16)


def depart(target, back, scores, jac_t, weight):
    return pl.pallas_call(
        depart_kernel,
        out_shape=jax.ShapeDtypeStruct(scores.shape, BF16),
        compiler_params=params(10), cost_estimate=took(3.5),
        name="depart",
    )(target, back, scores, jac_t, weight)


def ring(value, axis, move):
    count = lax.axis_size(axis)
    return lax.ppermute(value, axis, [(i, (i + move) % count) for i in range(count)])


def swapped(value):
    return lax.all_to_all(value, ("lat", "lon"), split_axis=0, concat_axis=0, tiled=True)


def shards(increment, courant, spectra, components, jacobian, obs_weight, tile_target, tile_cell):
    tiles = lax.axis_size("lat") * lax.axis_size("lon")
    count = spectra.shape[0]
    inc = increment.reshape(FEATS * ROWS, COLS)
    wind = courant.reshape(2 * LEVELS * ROWS, COLS)
    target = tile_target.reshape(1, count)
    cell = tile_cell
    jac_t = jacobian.T
    weight = obs_weight

    turned, low, high = lat_edges(inc, wind)
    south = ring(high, "lat", 1)
    north = ring(low, "lat", -1)
    total = begin(components, spectra.T, EARLY)
    total, south, north = lax.optimization_barrier((total, south, north))
    winds, low, high = lon_edges(turned, wind, south, north)
    west = ring(high, "lon", 1)
    east = ring(low, "lon", -1)
    scores, send = project(target, cell, components, spectra.T, total, EARLY, jac_t, weight, tiles)
    send, west, east = lax.optimization_barrier((send, west, east))
    got = swapped(send)
    coefs = weigh(winds, west, east)
    state = tangent(turned, south, north, west, east, coefs, jac_t, weight)

    send = gather(got, state)
    forcing, low, high = scatter(got, state)
    south = ring(high, "lat", 1)
    north = ring(low, "lat", -1)
    send, forcing = lax.optimization_barrier((send, forcing))
    back = swapped(send)
    low, winds = lax.optimization_barrier((low, winds))
    coefs = weigh(winds, west, east)
    low, high = forcing_edges(forcing, south, north)
    west = ring(high, "lon", 1)
    east = ring(low, "lon", -1)
    gradient = adjoint(inc, coefs, forcing, south, north, west, east)

    departures = depart(target, back, scores, jac_t, weight)
    return gradient.reshape(increment.shape), departures.T


def solution(mesh):
    placed = (
        P(None, None, "lat", "lon"),
        P(None, None, "lat", "lon"),
        P(("lat", "lon"), None),
        P(),
        P(),
        P(),
        P(("lat", "lon"), None),
        P(("lat", "lon")),
    )
    return jax.shard_map(
        shards,
        mesh=mesh,
        in_specs=placed,
        out_specs=(P(None, None, "lat", "lon"), P(("lat", "lon"), None)),
        check_vma=False,
    )
```
